128 devices in a mesh: expert: 32 (over z, y, core), dp: 4 (over x).
Axes of the slice: x: 4, y: 4, z: 4, core: 2. Of those that a mesh axis runs over, the one named last changes fastest.
Arguments:
- tokens: bfloat16 [16384, 2048], P(('expert', 'dp')), may hold values from -6 to 6
- cotangent: bfloat16 [16384, 2048], P(('expert', 'dp')), may hold values from -6 to 6
- route_ids: int32 [16384, 8], P(('expert', 'dp')), may hold values from 0 to 31, all different within a row; in each aligned block of 128 rows (0 to 127, 128 to 255, ...) at most 48 rows name the same one
- gate_probs: bfloat16 [16384, 8], P(('expert', 'dp')), may hold values from 0.019897461 to 0.5
- expert_rank: int32 [32], replicated, may hold values from 0 to 31, each once
- gate_kernel: bfloat16 [32, 2048, 768], P('expert'), may hold values from -0.125 to 0.125
- lift_kernel: bfloat16 [32, 2048, 768], P('expert'), may hold values from -0.125 to 0.125
- down_kernel: bfloat16 [32, 768, 2048], P('expert'), may hold values from -0.21875 to 0.21875
Outputs:
- tokens_grad: bfloat16 [16384, 2048], P(('expert', 'dp'))
- probs_grad: bfloat16 [16384, 8], P(('expert', 'dp'))
- gate_change: float32 [32, 2048, 768], P('expert', 'dp')
- lift_change: float32 [32, 2048, 768], P('expert', 'dp')
- down_change: float32 [32, 768, 2048], P('expert', None, 'dp')
The draws below stay inside these ranges and needn't reach their ends.
Inputs may be any that keep to these rules, and one draw needn't show every extreme that they name: `route_ids`: each token names 8 different experts; among the tokens of one device no expert is named more than 48 times. `expert_rank`: every expert once.
All inputs are finite; a program needn't handle non-finite values.
Results may differ from the reference program's by a relative error of at most 0.012.
Values may be sent and summed in bfloat16 or wider, within the bound.
A program may use at most 192 MiB of HBM per device.

```python
import math
import jax
import jax.numpy as jnp
import numpy as np
from jax import lax

D = 2048
FF = 768
TOP = 8
TOK_DEV = 128
EXPERTS = 32
TOKENS = 16384
CAP = 16
HALF = 8
SLOTS = 32
HOT = 16
MOST = 48
N_EXPERT = 32
N_DP = 4


def block_levels(own_key, extent, cuts, smallest, top_value):
    gain, own = 1.0, jax.random.fold_in(own_key, 6)
    for dim, parts in cuts:
        heights = jnp.exp(jax.random.uniform(jax.random.fold_in(own, dim), (parts,), jnp.float32, smallest / len(cuts), top_value / len(cuts)))
        gain = gain * jnp.repeat(heights, extent[dim] // parts).reshape([-1 if axis == dim else 1 for axis in range(len(extent))])
    return gain


def deal_out(key, own, number, rows, amount, top, bound, slope):
    ranking = jax.random.permutation(key, amount)
    crowded, ordinary = portions_of(amount, rows * top, bound, slope, True), portions_of(amount, rows * top, bound, slope, False)
    places = jnp.arange(amount)

    def named(tallies, rotation):
        used = int((tallies > 0).sum())
        fixed = max(1, used // 4)
        shifted = fixed + (places - fixed + rotation * (used - fixed)) % max(1, amount - fixed)
        return jnp.zeros((amount,), jnp.int32).at[ranking[jnp.where(places < fixed, places, shifted)]].set(jnp.asarray(tallies, jnp.int32))

    tallies = jnp.where(number % 4 == 0, named(crowded, number // 4), named(ordinary, number - number // 4 - 1))
    mixed = jax.random.permutation(jax.random.fold_in(own, 3), amount)
    donor, taker = mixed[0:amount // 2 * 2:2], mixed[1:amount // 2 * 2:2]
    margin = jnp.minimum(tallies[donor] - 1, bound - tallies[taker]) // 2
    margin = jnp.where((donor == ranking[0]) | (taker == ranking[0]) | (tallies[taker] == 0), 0, jnp.maximum(margin, 0))
    shifted = jax.random.randint(jax.random.fold_in(own, 4), (amount // 2,), 0, 1 << 20) % (margin + 1)
    tallies = tallies.at[donor].add(-shifted).at[taker].add(shifted)
    members = jnp.searchsorted(jnp.cumsum(tallies), jnp.arange(rows * top), side="right").astype(jnp.int32)
    table = members.reshape(top, rows).T
    table = table[jax.random.permutation(jax.random.fold_in(own, 1), rows)]
    rotation = jax.random.randint(jax.random.fold_in(own, 2), (rows, 1), 0, top)
    return jnp.take_along_axis(table, (jnp.arange(top)[None, :] + rotation) % top, axis=1)


def portions_of(number_of, total, reach, skew, full):
    weights = [(1 << 20) // math.isqrt(standing ** skew) + 1 for standing in range(1, number_of + 1)]
    largest = reach if full else min(reach, max(-(-total // number_of), total * weights[0] // sum(weights)))
    least = 1 if total - largest >= number_of - 1 else 0
    given, rest = [largest] + [least] * (number_of - 1), total - largest - least * (number_of - 1)
    while rest > 0:
        candidates = [i for i in range(1, number_of) if given[i] < largest] or [i for i in range(1, number_of) if given[i] < reach]
        whole, remaining = sum([weights[i] for i in candidates]), rest
        for i in candidates:
            addition = min(reach - given[i], max(1, remaining * weights[i] // whole), rest)
            given[i] = given[i] + addition
            rest = rest - addition
    return np.array(given)


def scatter_about(stream_key, dims, spread, reach, split=(), kind=jnp.bfloat16):
    values = spread * jax.random.normal(stream_key, dims, jnp.float32)
    if split:
        values = values * block_levels(stream_key, dims, split, -0.22, 0.18)
    return jnp.clip(values, -reach, reach).astype(kind)


def setup_inputs(seed: int = 0) -> dict:
    keys = jax.random.split(jax.random.key(seed), 9)
    tokens = scatter_about(keys[0], (TOKENS, D), 1.0, 6.0, ((0, 128),))
    cotangent = scatter_about(keys[1], (TOKENS, D), 1.0, 6.0, ((0, 128),))
    route_ids_keys = jax.random.split(jax.random.fold_in(keys[2], 1), TOKENS // TOK_DEV)
    route_ids_turns = jax.random.permutation(jax.random.fold_in(keys[2], 3), TOKENS // TOK_DEV)
    route_ids = jax.vmap(lambda own, number: deal_out(jax.random.fold_in(keys[2], 2), own, number, TOK_DEV, EXPERTS, TOP, MOST, 2))(route_ids_keys, route_ids_turns).reshape((TOKENS, TOP))
    gate_probs = jnp.clip(jnp.exp(math.log(0.5) - 3.224016 * jax.random.uniform(keys[3], (TOKENS, TOP), jnp.float32) ** block_levels(keys[3], (TOKENS, TOP), ((0, 128),), -0.2, 0.2)), 0.019897461, 0.5).astype(jnp.bfloat16)
    expert_rank = jax.random.permutation(keys[4], EXPERTS).astype(jnp.int32)
    gate_kernel = scatter_about(keys[5], (EXPERTS, D, FF), D ** -0.5, 0.125, ((0, 32),))
    lift_kernel = scatter_about(keys[6], (EXPERTS, D, FF), D ** -0.5, 0.125, ((0, 32),))
    down_kernel = scatter_about(keys[7], (EXPERTS, FF, D), FF ** -0.5, 0.21875, ((0, 32),))
    return {"tokens": tokens, "cotangent": cotangent, "route_ids": route_ids, "gate_probs": gate_probs, "expert_rank": expert_rank, "gate_kernel": gate_kernel, "lift_kernel": lift_kernel, "down_kernel": down_kernel}


def expert_pass(rows_x, rows_dy, rows_gate, kernel_gate, kernel_lift, kernel_down):
    gate_pre = jnp.dot(rows_x, kernel_gate, preferred_element_type=jnp.float32)
    lift_pre = jnp.dot(rows_x, kernel_lift, preferred_element_type=jnp.float32)
    sigmoid_part = jax.nn.sigmoid(gate_pre)
    activated = gate_pre * sigmoid_part
    hidden = (activated * lift_pre).astype(jnp.bfloat16)
    expert_out = jnp.dot(hidden, kernel_down, preferred_element_type=jnp.float32)
    prob_delta = jnp.sum(rows_dy.astype(jnp.float32) * expert_out, axis=-1).astype(jnp.bfloat16)
    scaled_cot = (rows_gate.astype(jnp.float32)[:, None] * rows_dy.astype(jnp.float32)).astype(jnp.bfloat16)
    contract_last = (((1,), (1,)), ((), ()))
    hidden_delta = lax.dot_general(scaled_cot, kernel_down, contract_last, preferred_element_type=jnp.float32)
    lift_delta = (hidden_delta * activated).astype(jnp.bfloat16)
    gate_delta = (hidden_delta * lift_pre * sigmoid_part * (1.0 + gate_pre * (1.0 - sigmoid_part))).astype(jnp.bfloat16)
    input_delta = lax.dot_general(gate_delta, kernel_gate, contract_last, preferred_element_type=jnp.float32)
    input_delta = input_delta + lax.dot_general(lift_delta, kernel_lift, contract_last, preferred_element_type=jnp.float32)
    return input_delta.astype(jnp.bfloat16), prob_delta, hidden, scaled_cot, gate_delta, lift_delta


def kernel_terms(rows_x, hidden, scaled_cot, gate_delta, lift_delta):
    contract_first = (((0,), (0,)), ((), ()))
    gate_term = lax.dot_general(rows_x, gate_delta, contract_first, preferred_element_type=jnp.float32)
    lift_term = lax.dot_general(rows_x, lift_delta, contract_first, preferred_element_type=jnp.float32)
    down_term = lax.dot_general(hidden, scaled_cot, contract_first, preferred_element_type=jnp.float32)
    return jnp.stack([gate_term, lift_term], axis=1), down_term


def reference(tokens, cotangent, route_ids, gate_probs, expert_rank, gate_kernel, lift_kernel, down_kernel):
    device_total = N_EXPERT * N_DP
    route_total = TOKENS * TOP
    per_device = TOK_DEV * TOP
    flat_routes = route_ids.reshape(device_total, per_device)
    expert_ids = jnp.arange(EXPERTS, dtype=jnp.int32)
    one_hot = (flat_routes[:, :, None] == expert_ids[None, None, :]).astype(jnp.int32)
    slot_index = jnp.sum((jnp.cumsum(one_hot, axis=1) - one_hot) * one_hot, axis=2)
    hot_table = jnp.any(expert_rank[:HOT][:, None] == expert_ids[None, :], axis=0)
    route_hot = hot_table[flat_routes]
    kept = (slot_index < CAP) | (route_hot & (slot_index < SLOTS))
    device_ids = jnp.arange(device_total, dtype=jnp.int32)[:, None]
    source_index = device_ids // N_DP
    group_of = device_ids % N_DP
    rows_each = N_DP * N_EXPERT * SLOTS
    position = ((flat_routes * N_DP + group_of) * N_EXPERT + source_index) * SLOTS + slot_index
    position = jnp.where(kept, position, EXPERTS * rows_each).reshape(route_total).astype(jnp.int32)
    route_numbers = jnp.arange(route_total, dtype=jnp.int32)
    route_of_row = jnp.full((EXPERTS * rows_each,), route_total, jnp.int32).at[position].set(route_numbers, mode="drop")
    route_of_row = route_of_row.reshape(EXPERTS, rows_each)
    padded_tokens = jnp.concatenate([tokens, jnp.zeros((1, D), tokens.dtype)], axis=0)
    padded_cot = jnp.concatenate([cotangent, jnp.zeros((1, D), cotangent.dtype)], axis=0)
    padded_probs = jnp.concatenate([gate_probs.reshape(route_total), jnp.zeros((1,), gate_probs.dtype)], axis=0)

    def part_rows(array, group_index, lower, upper):
        shaped = array.reshape(N_DP, N_EXPERT, SLOTS, array.shape[-1])
        return shaped[group_index, :, lower:upper].reshape(-1, array.shape[-1])

    def one_expert(packed):
        route_rows, kernel_gate, kernel_lift, kernel_down = packed
        token_rows = route_rows // TOP
        rows_x = padded_tokens[token_rows]
        rows_dy = padded_cot[token_rows]
        rows_gate = padded_probs[route_rows]
        input_delta, prob_delta, hidden, scaled_cot, gate_delta, lift_delta = expert_pass(rows_x, rows_dy, rows_gate, kernel_gate, kernel_lift, kernel_down)
        main_gate_lift = jnp.zeros((D, 2, FF), jnp.float32)
        main_down = jnp.zeros((FF, D), jnp.float32)
        far_gate_lift = jnp.zeros((D, 2, FF), jnp.float32)
        far_down = jnp.zeros((FF, D), jnp.float32)
        for group_index in range(N_DP):
            for lower, upper in ((0, CAP), (CAP, CAP + HALF), (CAP + HALF, SLOTS)):
                pieces = [part_rows(item, group_index, lower, upper) for item in (rows_x, hidden, scaled_cot, gate_delta, lift_delta)]
                gate_lift, down_term = kernel_terms(*pieces)
                rounded = lax.optimization_barrier((gate_lift.astype(jnp.bfloat16), down_term.astype(jnp.bfloat16)))
                if lower == CAP + HALF:
                    far_gate_lift = far_gate_lift + rounded[0].astype(jnp.float32)
                    far_down = far_down + rounded[1].astype(jnp.float32)
                else:
                    main_gate_lift = main_gate_lift + rounded[0].astype(jnp.float32)
                    main_down = main_down + rounded[1].astype(jnp.float32)
        far_rounded = lax.optimization_barrier((far_gate_lift.astype(jnp.bfloat16), far_down.astype(jnp.bfloat16)))
        gate_lift_total = main_gate_lift + far_rounded[0].astype(jnp.float32)
        down_total = main_down + far_rounded[1].astype(jnp.float32)
        return input_delta, prob_delta, gate_lift_total, down_total

    results = lax.map(one_expert, (route_of_row, gate_kernel, lift_kernel, down_kernel))
    input_flat = jnp.concatenate([results[0].reshape(-1, D), jnp.zeros((1, D), jnp.bfloat16)], axis=0)
    prob_flat = jnp.concatenate([results[1].reshape(-1), jnp.zeros((1,), jnp.bfloat16)], axis=0)
    per_route = input_flat[position].reshape(TOKENS, TOP, D)
    tokens_grad = jnp.sum(per_route, axis=1, dtype=jnp.float32).astype(jnp.bfloat16)
    probs_grad = prob_flat[position].reshape(TOKENS, TOP)
    gate_change = results[2][:, :, 0, :]
    lift_change = results[2][:, :, 1, :]
    down_change = results[3]
    return (tokens_grad, probs_grad, gate_change, lift_change, down_change)
```

```python
import jax
import jax.numpy as jnp
from jax import lax
from jax.sharding import PartitionSpec as P


def expert_pass(rows_x, scaled_cot, kernel_gate, kernel_lift, kernel_down):
    gate_pre = jnp.dot(rows_x, kernel_gate, preferred_element_type=jnp.float32)
    lift_pre = jnp.dot(rows_x, kernel_lift, preferred_element_type=jnp.float32)
    sigmoid_part = jax.nn.sigmoid(gate_pre)
    activated = gate_pre * sigmoid_part
    hidden = (activated * lift_pre).astype(jnp.bfloat16)
    expert_out = jnp.dot(hidden, kernel_down, preferred_element_type=jnp.float32)
    prob_delta = jnp.sum(scaled_cot.astype(jnp.float32) * expert_out, axis=-1).astype(jnp.bfloat16)
    contract_last = (((1,), (1,)), ((), ()))
    hidden_delta = lax.dot_general(
        scaled_cot, kernel_down, contract_last, preferred_element_type=jnp.float32
    )
    lift_delta = (hidden_delta * activated).astype(jnp.bfloat16)
    gate_delta = (
        hidden_delta * lift_pre * sigmoid_part * (1.0 + gate_pre * (1.0 - sigmoid_part))
    ).astype(jnp.bfloat16)
    input_delta = lax.dot_general(
        gate_delta, kernel_gate, contract_last, preferred_element_type=jnp.float32
    )
    input_delta = input_delta + lax.dot_general(
        lift_delta, kernel_lift, contract_last, preferred_element_type=jnp.float32
    )
    return (
        input_delta.astype(jnp.bfloat16),
        prob_delta,
        hidden,
        gate_delta,
        lift_delta,
    )


def kernel_terms(rows_x, hidden, scaled_cot, gate_delta, lift_delta):
    contract_first = (((0,), (0,)), ((), ()))
    gate_term = lax.dot_general(
        rows_x, gate_delta, contract_first, preferred_element_type=jnp.float32
    )
    lift_term = lax.dot_general(
        rows_x, lift_delta, contract_first, preferred_element_type=jnp.float32
    )
    down_term = lax.dot_general(
        hidden, scaled_cot, contract_first, preferred_element_type=jnp.float32
    )
    return (jnp.stack([gate_term, lift_term], axis=1), down_term)


def shards(
    tokens, cotangent, route_ids, gate_probs, expert_rank, gate_kernel, lift_kernel, down_kernel
):
    expert_count = lax.axis_size("expert")
    token_count, pick_count = route_ids.shape
    width = tokens.shape[1]
    capacity = token_count * pick_count // (2 * expert_count)
    slot_count = 2 * capacity
    expert_ids = jnp.arange(expert_count, dtype=jnp.int32)
    is_hot = jnp.any(expert_rank[: expert_count // 2, None] == expert_ids[None, :], axis=0)
    limit = jnp.where(is_hot, slot_count, capacity)
    named = route_ids[:, :, None] == expert_ids[None, None, :]
    chosen = jnp.any(named, axis=1)
    weight = jnp.sum(jnp.where(named, gate_probs.astype(jnp.float32)[:, :, None], 0.0), axis=1)
    below = jnp.tril(jnp.ones((token_count, token_count), jnp.bfloat16), -1)
    order = jnp.dot(below, chosen.astype(jnp.bfloat16), preferred_element_type=jnp.float32)
    order = order.astype(jnp.int32)
    held = chosen & (order < limit[None, :])
    pick = held[:, :, None] & (order[:, :, None] == jnp.arange(slot_count)[None, None, :])
    place = pick.astype(jnp.bfloat16).reshape(token_count, -1)
    scale = jnp.where(pick, weight[:, :, None], 0.0).astype(jnp.bfloat16)
    scale = scale.reshape(token_count, -1)
    contract_first = (((0,), (0,)), ((), ()))
    send_tokens = lax.dot_general(
        place, tokens, contract_first, preferred_element_type=jnp.float32
    ).astype(jnp.bfloat16)
    send_cot = lax.dot_general(
        scale, cotangent, contract_first, preferred_element_type=jnp.float32
    ).astype(jnp.bfloat16)
    rows_x = lax.all_to_all(send_tokens, "expert", split_axis=0, concat_axis=0, tiled=True)
    rows_sc = lax.all_to_all(send_cot, "expert", split_axis=0, concat_axis=0, tiled=True)
    own_kernels = (gate_kernel[0], lift_kernel[0], down_kernel[0])
    input_rows, prob_rows, hidden, gate_delta, lift_delta = expert_pass(
        rows_x, rows_sc, *own_kernels
    )
    gate_lift, down = kernel_terms(rows_x, hidden, rows_sc, gate_delta, lift_delta)
    gate_lift = lax.psum_scatter(
        gate_lift.astype(jnp.bfloat16), "dp", scatter_dimension=0, tiled=True
    ).astype(jnp.float32)
    down = lax.psum_scatter(
        down.astype(jnp.bfloat16), "dp", scatter_dimension=1, tiled=True
    ).astype(jnp.float32)
    back_rows = lax.all_to_all(input_rows, "expert", split_axis=0, concat_axis=0, tiled=True)
    back_probs = lax.all_to_all(
        prob_rows.reshape(expert_count, slot_count),
        "expert", split_axis=0, concat_axis=0, tiled=True,
    )
    tokens_grad = jnp.dot(place, back_rows, preferred_element_type=jnp.float32)
    by_expert = jnp.sum(
        jnp.where(pick, back_probs.astype(jnp.float32)[None], 0.0), axis=2
    )
    by_pick = jnp.sum(jnp.where(named, by_expert[:, None, :], 0.0), axis=2)
    probs_grad = (by_pick / gate_probs.astype(jnp.float32)).astype(jnp.bfloat16)
    return (
        tokens_grad.astype(jnp.bfloat16), probs_grad,
        gate_lift[:, 0][None], gate_lift[:, 1][None], down[None],
    )


def solution(mesh):
    return jax.shard_map(
        shards,
        mesh=mesh,
        in_specs=(
            P(("expert", "dp"), None),
            P(("expert", "dp"), None),
            P(("expert", "dp"), None),
            P(("expert", "dp"), None),
            P(),
            P("expert", None, None),
            P("expert", None, None),
            P("expert", None, None),
        ),
        out_specs=(
            P(("expert", "dp"), None),
            P(("expert", "dp"), None),
            P("expert", "dp", None),
            P("expert", "dp", None),
            P("expert", None, "dp"),
        ),
        check_vma=False,
    )
```

```python
import functools

import jax
import jax.numpy as jnp
from jax import lax
from jax.experimental import pallas as pl
from jax.experimental.pallas import tpu as pltpu
from jax.sharding import PartitionSpec as P

MESH = pl.DeviceIdType.MESH
NOTE = 128
FIRST = (((0,), (0,)), ((), ()))
LAST = (((1,), (1,)), ((), ()))
F32 = jnp.float32
BF16 = jnp.bfloat16


def dot(a, b, dims=(((1,), (0,)), ((), ()))):
    return lax.dot_general(a, b, dims, preferred_element_type=F32)


def layer_kernel(
    expert_count, group_count, slots, group_size,
    tokens, cotangent, routes, probs, rank, gate_hbm, lift_hbm, down_hbm,
    tokens_grad, probs_grad, gate_change, lift_change, down_change,
    rows_in, place, x_turned, hidden_turned, deltas, back_out, back_in, sums_gl, sums_down,
    out_sem, in_sem, back_out_sem, back_in_sem, kernel_sem,
    gl_out_sem, gl_in_sem, down_out_sem, down_in_sem,
):
    me, group = lax.axis_index("expert"), lax.axis_index("dp")
    token_count, width = tokens.shape
    pick_count = routes.shape[1]
    inner = hidden_turned.shape[0]
    row_count = expert_count * slots
    capacity = slots // 2
    quarter = width // group_count
    half_gl, half_down = quarter // 2, inner // 2
    chunk_rows = group_size * slots
    chunks = expert_count // group_size
    up, down = lax.rem(group + 1, group_count), lax.rem(group + group_count - 1, group_count)
    across = lax.rem(group + 2, group_count)

    def peer(step):
        return lax.rem(me + step, expert_count)

    barrier = pltpu.get_barrier_semaphore()

    @pl.loop(1, expert_count)
    def _(step):
        pl.semaphore_signal(barrier, inc=1, device_id=(peer(step), group), device_id_type=MESH)

    for neighbour in (up, down):
        pl.semaphore_signal(barrier, inc=1, device_id=(me, neighbour), device_id_type=MESH)

    lane = lax.broadcasted_iota(jnp.int32, (1, row_count), 1)
    lane_step = lax.shift_right_logical(lane, slots.bit_length() - 1)
    lane_expert = me + lane_step
    lane_expert = jnp.where(lane_expert >= expert_count, lane_expert - expert_count, lane_expert)
    lane_slot = lax.bitwise_and(lane, slots - 1).astype(F32)
    busy = jnp.where(rank[: expert_count // 2, :] == lane_expert, 1.0, 0.0)
    limit = capacity + (slots - capacity) * jnp.max(busy, axis=0, keepdims=True)
    gates = probs[...].astype(F32)
    chosen = jnp.zeros((token_count, row_count), F32)
    weight = jnp.zeros((token_count, row_count), F32)
    for pick in range(pick_count):
        hit = routes[:, pick : pick + 1] == lane_expert
        chosen = jnp.where(hit, 1.0, chosen)
        weight = jnp.where(hit, gates[:, pick : pick + 1], weight)
    below = jnp.where(
        lax.broadcasted_iota(jnp.int32, (token_count, token_count), 0)
        > lax.broadcasted_iota(jnp.int32, (token_count, token_count), 1),
        1.0,
        0.0,
    ).astype(BF16)
    order = dot(below, chosen.astype(BF16))
    kept = (chosen > 0.0) & (order == lane_slot) & (order < limit)
    place[...] = jnp.where(kept, 1.0, 0.0).astype(BF16)

    def first_part(rows_out, scale, gate, lift, down_kernel):
        loads = [
            pltpu.make_async_copy(source, target, kernel_sem.at[i])
            for i, (source, target) in enumerate(
                ((gate_hbm, gate), (lift_hbm, lift), (down_hbm, down_kernel))
            )
        ]
        for load in loads:
            load.start()
        scale[...] = jnp.where(kept, weight, 0.0).astype(BF16)

        def dispatch(step):
            return pltpu.make_async_remote_copy(
                src_ref=rows_out.at[step],
                dst_ref=rows_in.at[step],
                send_sem=out_sem.at[step],
                recv_sem=in_sem.at[step],
                device_id=(peer(step), group),
                device_id_type=MESH,
            )

        for part in range(chunks):
            columns = slice(part * chunk_rows, (part + 1) * chunk_rows)
            blocks = slice(part * group_size, (part + 1) * group_size)
            shape = (group_size, slots, width)
            rows_out[blocks, :slots, :] = (
                dot(place[:, columns], tokens[...], FIRST).astype(BF16).reshape(shape)
            )
            rows_out[blocks, slots:, :] = (
                dot(scale[:, columns], cotangent[...], FIRST).astype(BF16).reshape(shape)
            )
            if part == 0:
                rows_in[0] = rows_out[0]
                pl.semaphore_wait(barrier, expert_count + 1)

            @pl.loop(max(1, part * group_size), (part + 1) * group_size)
            def _(step):
                dispatch(step).start()

        for load in loads:
            load.wait()

        @pl.loop(0, chunks)
        def _(part):
            blocks = pl.ds(part * group_size, group_size)
            rows = pl.ds(pl.multiple_of(part * chunk_rows, chunk_rows), chunk_rows)

            @pl.loop(jnp.maximum(part * group_size, 1), (part + 1) * group_size)
            def _(step):
                dispatch(step).wait_recv()

            x = rows_in[blocks, :slots, :].reshape(chunk_rows, width)
            scaled = rows_in[blocks, slots:, :].reshape(chunk_rows, width)
            x_turned[:, rows] = x.T
            gate_pre = dot(x, gate[...])
            lift_pre = dot(x, lift[...])
            sigmoid = jax.nn.sigmoid(gate_pre)
            activated = gate_pre * sigmoid
            hidden = (activated * lift_pre).astype(BF16)
            hidden_turned[:, rows] = hidden.T
            expert_out = dot(hidden, down_kernel[...])
            prob = jnp.sum(scaled.astype(F32) * expert_out, axis=1, keepdims=True)
            back_out[blocks, :, width:] = (
                jnp.broadcast_to(prob, (chunk_rows, NOTE))
                .astype(BF16)
                .reshape(group_size, slots, NOTE)
            )
            hidden_delta = dot(scaled, down_kernel[...], LAST)
            lift_delta = (hidden_delta * activated).astype(BF16)
            gate_delta = (
                hidden_delta * lift_pre * sigmoid * (1.0 + gate_pre * (1.0 - sigmoid))
            ).astype(BF16)
            deltas[rows, :inner] = gate_delta
            deltas[rows, inner:] = lift_delta
            route_delta = dot(gate_delta, gate[...], LAST) + dot(lift_delta, lift[...], LAST)
            back_out[blocks, :, :width] = route_delta.astype(BF16).reshape(
                group_size, slots, width
            )

        @pl.loop(1, expert_count)
        def _(step):
            dispatch(step).wait_send()

    kernel_shape = gate_hbm.shape
    pl.run_scoped(
        first_part,
        pltpu.VMEM((expert_count, 2 * slots, width), BF16),
        pltpu.VMEM((token_count, row_count), BF16),
        pltpu.VMEM(kernel_shape, BF16),
        pltpu.VMEM(kernel_shape, BF16),
        pltpu.VMEM((inner, width), BF16),
    )

    def give_back(step):
        return pltpu.make_async_remote_copy(
            src_ref=back_out.at[step],
            dst_ref=back_in.at[step],
            send_sem=back_out_sem.at[step],
            recv_sem=back_in_sem.at[step],
            device_id=(lax.rem(me - step + expert_count, expert_count), group),
            device_id_type=MESH,
        )

    def term_gl(part, half):
        rows = pl.ds(pl.multiple_of(part * quarter + half * half_gl, half_gl), half_gl)
        return dot(x_turned[rows, :], deltas[...])

    def term_down(part, half):
        columns = pl.ds(pl.multiple_of(part * quarter, quarter), quarter)
        scaled = rows_in[:, slots:, columns].reshape(row_count, quarter)
        return dot(hidden_turned[half * half_down : (half + 1) * half_down, :], scaled)

    def second_part(partial_gl, partial_down):
        plan = (
            (across, 0, down, None),
            (across, 1, up, None),
            (up, 0, up, None),
            (down, 1, down, None),
            (down, 0, down, 0),
            (up, 1, up, 1),
        )

        def pass_on(number, kind):
            source, sink, send, receive = (
                (partial_gl, sums_gl, gl_out_sem, gl_in_sem),
                (partial_down, sums_down, down_out_sem, down_in_sem),
            )[kind]
            return pltpu.make_async_remote_copy(
                src_ref=source.at[number],
                dst_ref=sink.at[number],
                send_sem=send.at[number],
                recv_sem=receive.at[number],
                device_id=(me, plan[number][2]),
                device_id_type=MESH,
            )

        for number, (part, half, _, taken) in enumerate(plan):
            term = term_gl(part, half)
            if taken is not None:
                pass_on(taken, 0).wait_recv()
                term = term + sums_gl[taken].astype(F32)
            partial_gl[number] = term.astype(BF16)
            pass_on(number, 0).start()
            term = term_down(part, half)
            if taken is not None:
                pass_on(taken, 1).wait_recv()
                term = term + sums_down[taken].astype(F32)
            partial_down[number] = term.astype(BF16)
            pass_on(number, 1).start()
            if number == 1:

                @pl.loop(1, expert_count)
                def _(step):
                    give_back(step).start()

        for half in range(2):
            rows = slice(half * half_gl, (half + 1) * half_gl)
            term = term_gl(group, half)
            gate_change[0, rows, :] = term[:, :inner]
            lift_change[0, rows, :] = term[:, inner:]
            rows = slice(half * half_down, (half + 1) * half_down)
            down_change[0, rows, :] = term_down(group, half)

        back_in[0] = back_out[0]

        @pl.loop(1, expert_count)
        def _(step):
            give_back(step).wait_recv()

        returned = back_in[:, :, :width].reshape(row_count, width)
        tokens_grad[...] = dot(place[...], returned).astype(BF16)
        notes = back_in[:, :, width:].reshape(row_count, NOTE)
        note_row = lax.broadcasted_iota(jnp.int32, (row_count, NOTE), 0)
        note_lane = lax.broadcasted_iota(jnp.int32, (row_count, NOTE), 1)
        note_step = lax.shift_right_logical(note_row, slots.bit_length() - 1)
        notes = jnp.where(note_step == note_lane, notes.astype(F32), 0.0).astype(BF16)
        by_step = dot(place[...], notes)
        token_lane = lax.broadcasted_iota(jnp.int32, (token_count, NOTE), 1)
        pick_lane = lax.broadcasted_iota(jnp.int32, (token_count, pick_count), 1)
        total = jnp.zeros((token_count, pick_count), F32)
        for pick in range(pick_count):
            step = routes[:, pick : pick + 1] - me
            step = jnp.where(step < 0, step + expert_count, step)
            value = jnp.sum(jnp.where(token_lane == step, by_step, 0.0), axis=1, keepdims=True)
            total = jnp.where(pick_lane == pick, value, total)
        probs_grad[...] = (total / probs[...].astype(F32)).astype(BF16)

        for half, numbers in ((0, (2, 4)), (1, (3, 5))):
            rows = slice(half * half_gl, (half + 1) * half_gl)
            for number in numbers:
                pass_on(number, 0).wait_recv()
                gate_change[0, rows, :] += sums_gl[number, :, :inner].astype(F32)
                lift_change[0, rows, :] += sums_gl[number, :, inner:].astype(F32)
            rows = slice(half * half_down, (half + 1) * half_down)
            for number in numbers:
                pass_on(number, 1).wait_recv()
                down_change[0, rows, :] += sums_down[number].astype(F32)

        for number in range(len(plan)):
            for kind in range(2):
                pass_on(number, kind).wait_send()

        @pl.loop(1, expert_count)
        def _(step):
            give_back(step).wait_send()

    pl.run_scoped(
        second_part,
        pltpu.VMEM((6, half_gl, 2 * inner), BF16),
        pltpu.VMEM((6, half_down, quarter), BF16),
    )


def shards(
    tokens, cotangent, route_ids, gate_probs, expert_rank, gate_kernel, lift_kernel, down_kernel
):
    expert_count = lax.axis_size("expert")
    group_count = lax.axis_size("dp")
    token_count, pick_count = route_ids.shape
    width = tokens.shape[1]
    inner = gate_kernel.shape[2]
    slots = token_count * pick_count // expert_count
    row_count = expert_count * slots
    quarter = width // group_count
    group_size = max(1, expert_count // 4)
    flops = 2 * row_count * width * inner * 9
    vmem, anywhere = pl.BlockSpec(memory_space=pltpu.VMEM), pl.BlockSpec(memory_space=pl.ANY)
    dma = pltpu.SemaphoreType.DMA
    return pl.pallas_call(
        functools.partial(layer_kernel, expert_count, group_count, slots, group_size),
        out_shape=(
            jax.ShapeDtypeStruct(tokens.shape, BF16),
            jax.ShapeDtypeStruct(gate_probs.shape, BF16),
            jax.ShapeDtypeStruct((1, quarter, inner), F32),
            jax.ShapeDtypeStruct((1, quarter, inner), F32),
            jax.ShapeDtypeStruct((1, inner, quarter), F32),
        ),
        in_specs=[vmem] * 5 + [anywhere] * 3,
        out_specs=[vmem] * 5,
        scratch_shapes=[
            pltpu.VMEM((expert_count, 2 * slots, width), BF16),
            pltpu.VMEM((token_count, row_count), BF16),
            pltpu.VMEM((width, row_count), BF16),
            pltpu.VMEM((inner, row_count), BF16),
            pltpu.VMEM((row_count, 2 * inner), BF16),
            pltpu.VMEM((expert_count, slots, width + NOTE), BF16),
            pltpu.VMEM((expert_count, slots, width + NOTE), BF16),
            pltpu.VMEM((6, quarter // 2, 2 * inner), BF16),
            pltpu.VMEM((6, inner // 2, quarter), BF16),
            dma((expert_count,)),
            dma((expert_count,)),
            dma((expert_count,)),
            dma((expert_count,)),
            dma((3,)),
            dma((6,)),
            dma((6,)),
            dma((6,)),
            dma((6,)),
        ],
        compiler_params=pltpu.CompilerParams(
            collective_id=0, has_side_effects=True, vmem_limit_bytes=64 * 1024 * 1024
        ),
        cost_estimate=pl.CostEstimate(
            flops=flops, bytes_accessed=16 * 1024 * 1024, transcendentals=row_count * inner
        ),
    )(
        tokens,
        cotangent,
        route_ids,
        gate_probs,
        expert_rank.reshape(expert_count, 1),
        gate_kernel[0],
        lift_kernel[0],
        down_kernel[0],
    )


def solution(mesh):
    return jax.shard_map(
        shards,
        mesh=mesh,
        in_specs=(
            P(("expert", "dp"), None),
            P(("expert", "dp"), None),
            P(("expert", "dp"), None),
            P(("expert", "dp"), None),
            P(),
            P("expert", None, None),
            P("expert", None, None),
            P("expert", None, None),
        ),
        out_specs=(
            P(("expert", "dp"), None),
            P(("expert", "dp"), None),
            P("expert", "dp", None),
            P("expert", "dp", None),
            P("expert", None, "dp"),
        ),
        check_vma=False,
    )
```

```python
import functools

import jax
import jax.numpy as jnp
from jax import lax
from jax.experimental import pallas as pl
from jax.experimental.pallas import tpu as pltpu
from jax.sharding import PartitionSpec as P

MESH = pl.DeviceIdType.MESH
NOTE = 128
FIRST = (((0,), (0,)), ((), ()))
LAST = (((1,), (1,)), ((), ()))
F32 = jnp.float32
BF16 = jnp.bfloat16


def dot(a, b, dims=(((1,), (0,)), ((), ()))):
    return lax.dot_general(a, b, dims, preferred_element_type=F32)


ORDER = (0, 1, 3, 2)
PAIRS = tuple(
    sorted(
        ((dz, dy) for dz in ORDER for dy in ORDER),
        key=lambda pair: (max(ORDER.index(pair[0]), ORDER.index(pair[1])), pair),
    )
)
SIDE = 4
CORES = 2
STEPS = (1, 3)


def layer_kernel(
    expert_count, group_count, slots, pick_count,
    tokens, cotangent, meta, gate_hbm, lift_hbm, down_hbm,
    tokens_grad, probs_grad, gate_change, lift_change, down_change,
    line_rows, line_meta, relayed, rows_in, place, x_turned, hidden_turned, deltas,
    back_out, back_in, sums_gl, sums_down,
    line_out_sem, line_in_sem, near_out_sem, near_in_sem, side_out_sem, side_in_sem,
    relay_out_sem, relay_in_sem, last_out_sem, last_in_sem, back_out_sem, back_in_sem, kernel_sem,
    gl_out_sem, gl_in_sem, down_out_sem, down_in_sem,
):
    me, group = lax.axis_index("expert"), lax.axis_index("dp")
    token_count, width = tokens.shape
    wide = width // 2
    inner = hidden_turned.shape[0]
    row_count = expert_count * slots
    quarter = width // group_count
    half_gl, half_down = quarter // 2, inner // 2
    chunk_pairs = len(PAIRS) // 4
    chunk_rows = chunk_pairs * CORES * slots
    up, down = (group + 1) % group_count, (group + group_count - 1) % group_count
    across = (group + 2) % group_count
    my_z, my_y, my_core = me // (SIDE * CORES), (me // CORES) % SIDE, me % CORES

    def device(dz, dy, core):
        z, y = (my_z + dz) % SIDE, (my_y + dy) % SIDE
        return (z * SIDE + y) * CORES + (my_core + core) % CORES

    def along(half, offset, core):
        return device(0, offset, core) if half == 0 else device(offset, 0, core)

    def pair_of(half, part, offset):
        offset %= SIDE
        return PAIRS.index((part, offset) if half == 0 else (offset, part))

    barrier = pltpu.get_barrier_semaphore()

    @pl.loop(1, expert_count)
    def _(step):
        pl.semaphore_signal(
            barrier, inc=1, device_id=((me + step) % expert_count, group), device_id_type=MESH
        )

    for neighbour in (up, down):
        pl.semaphore_signal(barrier, inc=1, device_id=(me, neighbour), device_id_type=MESH)

    def remote(source, target, send, receive, expert):
        return pltpu.make_async_remote_copy(
            src_ref=source,
            dst_ref=target,
            send_sem=send,
            recv_sem=receive,
            device_id=(expert, group),
            device_id_type=MESH,
        )

    def line_own(half, way, kind):
        columns = slice(half * wide, (half + 1) * wide)
        source = (tokens.at[:, columns], cotangent.at[:, columns], meta)[kind]
        slot = -STEPS[way] % SIDE - 1
        target = line_meta.at[half, slot] if kind == 2 else line_rows.at[half, slot, kind]
        return remote(
            source, target, line_out_sem.at[half, way, kind], line_in_sem.at[half, slot, kind],
            along(1 - half, STEPS[way], 0),
        )

    def line_on(half, kind):
        way = 1 if kind == 1 else 0
        slot = -STEPS[way] % SIDE - 1
        if kind == 2:
            source, target = line_meta.at[half, slot], line_meta.at[half, 1]
        else:
            source, target = line_rows.at[half, slot, kind], line_rows.at[half, 1, kind]
        return remote(
            source, target, line_out_sem.at[half, 2, kind], line_in_sem.at[half, 1, kind],
            along(1 - half, STEPS[way], 0),
        )

    def near(half, part, way, core, rows_out):
        offset = STEPS[way]
        return remote(
            rows_out.at[half, ORDER.index(part) % 2, offset, :, core],
            rows_in.at[half, pair_of(half, part, -offset), core],
            near_out_sem.at[half, part, way, core], near_in_sem.at[half, part, way, core],
            along(half, offset, core),
        )

    def beside(half, part, rows_out):
        return remote(
            rows_out.at[half, ORDER.index(part) % 2, 0, :, 1],
            rows_in.at[half, pair_of(half, part, 0), 1],
            side_out_sem.at[half, part], side_in_sem.at[half, part],
            along(half, 0, 1),
        )

    def relay(half, part, way, rows_out):
        return remote(
            rows_out.at[half, ORDER.index(part) % 2, 2, way],
            relayed.at[half, way, part],
            relay_out_sem.at[half, part, way], relay_in_sem.at[half, part, way],
            along(half, STEPS[way], 0),
        )

    def last(half, part, way, core):
        return remote(
            relayed.at[half, way, part, core],
            rows_in.at[half, pair_of(half, part, 2), core, way],
            last_out_sem.at[half, part, way, core], last_in_sem.at[half, part, way, core],
            along(half, STEPS[way], core),
        )

    def sends_of(half, part, rows_out):
        return (
            [beside(half, part, rows_out)]
            + [relay(half, part, way, rows_out) for way in range(2)]
            + [near(half, part, way, core, rows_out) for way in range(2) for core in range(CORES)]
        )

    below = jnp.where(
        lax.broadcasted_iota(jnp.int32, (token_count, token_count), 0)
        > lax.broadcasted_iota(jnp.int32, (token_count, token_count), 1),
        1.0,
        0.0,
    ).astype(BF16)
    shift = slots.bit_length() - 1

    def tables(facts, experts):
        lanes = len(experts) * slots
        lane = lax.broadcasted_iota(jnp.int32, (1, lanes), 1)
        block = lax.shift_right_logical(lane, shift)
        slot = lax.bitwise_and(lane, slots - 1).astype(F32)
        named = jnp.zeros((1, lanes), jnp.int32)
        for number, expert in enumerate(experts):
            named = jnp.where(block == number, expert, named)
        named = named.astype(F32)
        facts = facts.astype(F32)
        limit = jnp.zeros((token_count, lanes), F32)
        weight = jnp.zeros((token_count, lanes), F32)
        for pick in range(pick_count):
            hit = facts[:, pick : pick + 1] == named
            weight = jnp.where(hit, facts[:, pick_count + pick : pick_count + pick + 1], weight)
            first = 2 * pick_count + pick
            limit = jnp.where(hit, facts[:, first : first + 1], limit)
        order = dot(below, jnp.where(limit > 0.0, 1.0, 0.0).astype(BF16))
        kept = (order == slot) & (order < limit)
        return (
            jnp.where(kept, 1.0, 0.0).astype(BF16),
            jnp.where(kept, weight, 0.0).astype(BF16),
        )

    def first_part(rows_out, gate, lift, down_kernel):
        loads = [
            pltpu.make_async_copy(source, target, kernel_sem.at[i])
            for i, (source, target) in enumerate(
                ((gate_hbm, gate), (lift_hbm, lift), (down_hbm, down_kernel))
            )
        ]
        for load in loads:
            load.start()
        pl.semaphore_wait(barrier, expert_count + 1)
        for kind in (2, 0, 1):
            for way in range(2):
                for half in range(2):
                    line_own(half, way, kind).start()

        line_experts = [
            [along(half, offset, core) for offset in range(SIDE) for core in range(CORES)]
            for half in range(2)
        ]

        def send_part(part):
            for half in range(2):
                number = ORDER.index(part)
                if part == 0:
                    columns = slice(half * wide, (half + 1) * wide)
                    sources = (tokens[:, columns], cotangent[:, columns])
                    facts = meta[...]
                else:
                    sources = (line_rows[half, part - 1, 0], line_rows[half, part - 1, 1])
                    facts = line_meta[half, part - 1]
                if number >= 2:
                    for copy in sends_of(half, ORDER[number - 2], rows_out):
                        copy.wait_send()
                for kind, table in enumerate(tables(facts, line_experts[half])):
                    chosen = dot(table, sources[kind], FIRST).astype(BF16)
                    chosen = chosen.reshape(SIDE, CORES, slots, wide)
                    rows_out[half, number % 2, :, kind] = chosen
                    rows_in[half, pair_of(half, part, 0), 0, kind] = chosen[0, 0]
                for copy in sends_of(half, part, rows_out):
                    copy.start()

        def pass_last(part):
            for half in range(2):
                for way in range(2):
                    relay(half, part, way, rows_out).wait_recv()
                    for core in range(CORES):
                        last(half, part, way, core).start()

        send_part(0)
        for half in range(2):
            for kind in (2, 0, 1):
                line_own(half, 0, kind).wait_recv()
                line_own(half, 1, kind).wait_recv()
                line_on(half, kind).start()
        send_part(1)
        pass_last(0)
        send_part(3)
        pass_last(1)
        for half in range(2):
            for kind in range(3):
                line_on(half, kind).wait_recv()
        send_part(2)
        place[...] = tables(
            meta[...], [device(-dz, -dy, core) for dz, dy in PAIRS for core in range(CORES)]
        )[0]
        pass_last(3)
        for load in loads:
            load.wait()

        def await_rows(half, part, offset):
            if offset == 0:
                beside(half, part, rows_out).wait_recv()
            for core in range(CORES):
                if offset == 2:
                    for way in range(2):
                        last(half, part, way, core).wait_recv()
                elif offset:
                    near(half, part, 1 - STEPS.index(offset), core, rows_out).wait_recv()

        @pl.loop(0, len(PAIRS) // chunk_pairs)
        def _(part):
            blocks = pl.ds(part * chunk_pairs, chunk_pairs)
            rows = pl.ds(pl.multiple_of(part * chunk_rows, chunk_rows), chunk_rows)
            for number in range(len(PAIRS) // chunk_pairs):

                @pl.when(part == number)
                def _():
                    if number == 2:
                        pass_last(2)
                    for dz, dy in PAIRS[number * chunk_pairs : (number + 1) * chunk_pairs]:
                        await_rows(0, dz, dy)
                        await_rows(1, dy, dz)

            x, scaled = (
                jnp.concatenate(
                    [rows_in[half, blocks, :, kind].reshape(chunk_rows, wide) for half in range(2)],
                    axis=1,
                )
                for kind in range(2)
            )
            shape = (chunk_pairs * CORES, slots)
            blocks = pl.ds(part * chunk_pairs * CORES, chunk_pairs * CORES)
            x_turned[:, rows] = x.T
            gate_pre = dot(x, gate[...])
            lift_pre = dot(x, lift[...])
            sigmoid = jax.nn.sigmoid(gate_pre)
            activated = gate_pre * sigmoid
            hidden = (activated * lift_pre).astype(BF16)
            hidden_turned[:, rows] = hidden.T
            expert_out = dot(hidden, down_kernel[...])
            prob = jnp.sum(scaled.astype(F32) * expert_out, axis=1, keepdims=True)
            back_out[blocks, :, width:] = (
                jnp.broadcast_to(prob, (chunk_rows, NOTE)).astype(BF16).reshape(*shape, NOTE)
            )
            hidden_delta = dot(scaled, down_kernel[...], LAST)
            lift_delta = (hidden_delta * activated).astype(BF16)
            gate_delta = (
                hidden_delta * lift_pre * sigmoid * (1.0 + gate_pre * (1.0 - sigmoid))
            ).astype(BF16)
            deltas[rows, :inner] = gate_delta
            deltas[rows, inner:] = lift_delta
            route_delta = dot(gate_delta, gate[...], LAST) + dot(lift_delta, lift[...], LAST)
            back_out[blocks, :, :width] = route_delta.astype(BF16).reshape(*shape, width)

        for half in range(2):
            for kind in range(3):
                for way in range(2):
                    line_own(half, way, kind).wait_send()
                line_on(half, kind).wait_send()
            for part in ORDER:
                if part in ORDER[2:]:
                    for copy in sends_of(half, part, rows_out):
                        copy.wait_send()
                for way in range(2):
                    for core in range(CORES):
                        last(half, part, way, core).wait_send()

    kernel_shape = gate_hbm.shape
    pl.run_scoped(
        first_part,
        pltpu.VMEM((2, 2, SIDE, 2, CORES, slots, wide), BF16),
        pltpu.VMEM(kernel_shape, BF16),
        pltpu.VMEM(kernel_shape, BF16),
        pltpu.VMEM((inner, width), BF16),
    )

    def give_back(step):
        dz, dy = PAIRS[step // CORES]
        return remote(
            back_out.at[step], back_in.at[step], back_out_sem.at[step], back_in_sem.at[step],
            device(dz, dy, step % CORES),
        )

    def term_gl(part, half):
        rows = pl.ds(pl.multiple_of(part * quarter + half * half_gl, half_gl), half_gl)
        return dot(x_turned[rows, :], deltas[...])

    def term_down(part, half):
        fraction = wide // quarter
        columns = pl.ds(pl.multiple_of((part % fraction) * quarter, quarter), quarter)
        scaled = rows_in[part // fraction, :, :, 1, :, columns].reshape(row_count, quarter)
        return dot(hidden_turned[half * half_down : (half + 1) * half_down, :], scaled)

    def second_part(partial_gl, partial_down):
        plan = (
            (across, 0, down, None),
            (across, 1, up, None),
            (up, 0, up, None),
            (down, 1, down, None),
            (down, 0, down, 0),
            (up, 1, up, 1),
        )

        def pass_on(number, kind):
            source, sink, send, receive = (
                (partial_gl, sums_gl, gl_out_sem, gl_in_sem),
                (partial_down, sums_down, down_out_sem, down_in_sem),
            )[kind]
            return pltpu.make_async_remote_copy(
                src_ref=source.at[number],
                dst_ref=sink.at[number],
                send_sem=send.at[number],
                recv_sem=receive.at[number],
                device_id=(me, plan[number][2]),
                device_id_type=MESH,
            )

        for number, (part, half, _, taken) in enumerate(plan):
            term = term_gl(part, half)
            if taken is not None:
                pass_on(taken, 0).wait_recv()
                term = term + sums_gl[taken].astype(F32)
            partial_gl[number] = term.astype(BF16)
            pass_on(number, 0).start()
            term = term_down(part, half)
            if taken is not None:
                pass_on(taken, 1).wait_recv()
                term = term + sums_down[taken].astype(F32)
            partial_down[number] = term.astype(BF16)
            pass_on(number, 1).start()
            if number == 1:
                for step in range(1, expert_count):
                    give_back(step).start()

        for half in range(2):
            rows = slice(half * half_gl, (half + 1) * half_gl)
            term = term_gl(group, half)
            gate_change[0, rows, :] = term[:, :inner]
            lift_change[0, rows, :] = term[:, inner:]
            rows = slice(half * half_down, (half + 1) * half_down)
            down_change[0, rows, :] = term_down(group, half)

        back_in[0] = back_out[0]

        for step in range(1, expert_count):
            give_back(step).wait_recv()

        returned = back_in[:, :, :width].reshape(row_count, width)
        tokens_grad[...] = dot(place[...], returned).astype(BF16)
        notes = back_in[:, :, width:].reshape(row_count, NOTE)
        note_row = lax.broadcasted_iota(jnp.int32, (row_count, NOTE), 0)
        note_lane = lax.broadcasted_iota(jnp.int32, (row_count, NOTE), 1)
        note_step = lax.shift_right_logical(note_row, slots.bit_length() - 1)
        notes = jnp.where(note_step == note_lane, notes.astype(F32), 0.0).astype(BF16)
        by_step = dot(place[...], notes)
        note_lane = lax.broadcasted_iota(jnp.int32, (1, NOTE), 1)
        sender = jnp.full((1, NOTE), -1, jnp.int32)
        for number in range(expert_count):
            dz, dy = PAIRS[number // CORES]
            sender = jnp.where(note_lane == number, device(-dz, -dy, number % CORES), sender)
        sender = sender.astype(F32)
        facts = meta[...].astype(F32)
        pick_lane = lax.broadcasted_iota(jnp.int32, (token_count, pick_count), 1)
        total = jnp.zeros((token_count, pick_count), F32)
        for pick in range(pick_count):
            value = jnp.where(facts[:, pick : pick + 1] == sender, by_step, 0.0)
            value = jnp.sum(value, axis=1, keepdims=True)
            total = jnp.where(pick_lane == pick, value, total)
        probs_grad[...] = (total / facts[:, pick_count : 2 * pick_count]).astype(BF16)

        for half, numbers in ((0, (2, 4)), (1, (3, 5))):
            rows = slice(half * half_gl, (half + 1) * half_gl)
            for number in numbers:
                pass_on(number, 0).wait_recv()
                gate_change[0, rows, :] += sums_gl[number, :, :inner].astype(F32)
                lift_change[0, rows, :] += sums_gl[number, :, inner:].astype(F32)
            rows = slice(half * half_down, (half + 1) * half_down)
            for number in numbers:
                pass_on(number, 1).wait_recv()
                down_change[0, rows, :] += sums_down[number].astype(F32)

        for number in range(len(plan)):
            for kind in range(2):
                pass_on(number, kind).wait_send()

        for step in range(1, expert_count):
            give_back(step).wait_send()

    pl.run_scoped(
        second_part,
        pltpu.VMEM((6, half_gl, 2 * inner), BF16),
        pltpu.VMEM((6, half_down, quarter), BF16),
    )


def shards(
    tokens, cotangent, route_ids, gate_probs, expert_rank, gate_kernel, lift_kernel, down_kernel
):
    expert_count = lax.axis_size("expert")
    group_count = lax.axis_size("dp")
    token_count, pick_count = route_ids.shape
    width = tokens.shape[1]
    inner = gate_kernel.shape[2]
    slots = token_count * pick_count // expert_count
    row_count = expert_count * slots
    quarter = width // group_count
    hot = jnp.any(route_ids[:, :, None] == expert_rank[: expert_count // 2], axis=2)
    limit = jnp.where(hot, slots, slots // 2)
    meta = jnp.concatenate([route_ids.astype(BF16), gate_probs, limit.astype(BF16)], axis=1)
    meta = jnp.pad(meta, ((0, 0), (0, NOTE - meta.shape[1])))
    vmem, anywhere = pl.BlockSpec(memory_space=pltpu.VMEM), pl.BlockSpec(memory_space=pl.ANY)
    dma = pltpu.SemaphoreType.DMA
    return pl.pallas_call(
        functools.partial(layer_kernel, expert_count, group_count, slots, pick_count),
        out_shape=(
            jax.ShapeDtypeStruct(tokens.shape, BF16),
            jax.ShapeDtypeStruct(gate_probs.shape, BF16),
            jax.ShapeDtypeStruct((1, quarter, inner), F32),
            jax.ShapeDtypeStruct((1, quarter, inner), F32),
            jax.ShapeDtypeStruct((1, inner, quarter), F32),
        ),
        in_specs=[vmem] * 3 + [anywhere] * 3,
        out_specs=[vmem] * 5,
        scratch_shapes=[
            pltpu.VMEM((2, SIDE - 1, 2, token_count, width // 2), BF16),
            pltpu.VMEM((2, SIDE - 1, token_count, NOTE), BF16),
            pltpu.VMEM((2, 2, SIDE, CORES, slots, width // 2), BF16),
            pltpu.VMEM((2, len(PAIRS), CORES, 2, slots, width // 2), BF16),
            pltpu.VMEM((token_count, row_count), BF16),
            pltpu.VMEM((width, row_count), BF16),
            pltpu.VMEM((inner, row_count), BF16),
            pltpu.VMEM((row_count, 2 * inner), BF16),
            pltpu.VMEM((expert_count, slots, width + NOTE), BF16),
            pltpu.VMEM((expert_count, slots, width + NOTE), BF16),
            pltpu.VMEM((6, quarter // 2, 2 * inner), BF16),
            pltpu.VMEM((6, inner // 2, quarter), BF16),
            dma((2, 3, 3)),
            dma((2, 3, 3)),
            dma((2, SIDE, 2, CORES)),
            dma((2, SIDE, 2, CORES)),
            dma((2, SIDE)),
            dma((2, SIDE)),
            dma((2, SIDE, 2)),
            dma((2, SIDE, 2)),
            dma((2, SIDE, 2, CORES)),
            dma((2, SIDE, 2, CORES)),
            dma((expert_count,)),
            dma((expert_count,)),
            dma((3,)),
            dma((6,)),
            dma((6,)),
            dma((6,)),
            dma((6,)),
        ],
        compiler_params=pltpu.CompilerParams(
            collective_id=0, has_side_effects=True, vmem_limit_bytes=64 * 1024 * 1024
        ),
        cost_estimate=pl.CostEstimate(
            flops=18 * row_count * width * inner,
            bytes_accessed=16 * 1024 * 1024,
            transcendentals=row_count * inner,
        ),
    )(tokens, cotangent, meta, gate_kernel[0], lift_kernel[0], down_kernel[0])


def solution(mesh):
    return jax.shard_map(
        shards,
        mesh=mesh,
        in_specs=(
            P(("expert", "dp"), None),
            P(("expert", "dp"), None),
            P(("expert", "dp"), None),
            P(("expert", "dp"), None),
            P(),
            P("expert", None, None),
            P("expert", None, None),
            P("expert", None, None),
        ),
        out_specs=(
            P(("expert", "dp"), None),
            P(("expert", "dp"), None),
            P("expert", "dp", None),
            P("expert", "dp", None),
            P("expert", None, "dp"),
        ),
        check_vma=False,
    )
```

```python
import functools

import jax
import jax.numpy as jnp
from jax import lax
from jax.experimental import pallas as pl
from jax.experimental.pallas import tpu as pltpu
from jax.sharding import PartitionSpec as P

MESH = pl.DeviceIdType.MESH
NOTE = 128
FIRST = (((0,), (0,)), ((), ()))
LAST = (((1,), (1,)), ((), ()))
F32 = jnp.float32
BF16 = jnp.bfloat16


def dot(a, b, dims=(((1,), (0,)), ((), ()))):
    return lax.dot_general(a, b, dims, preferred_element_type=F32)


ORDER = (0, 1, 3, 2)
PAIRS = tuple(
    sorted(
        ((dz, dy) for dz in ORDER for dy in ORDER),
        key=lambda pair: sorted((ORDER.index(pair[0]), ORDER.index(pair[1])), reverse=True),
    )
)
SIDE = 4
CORES = 2
STEPS = (1, 3)


def layer_kernel(
    expert_count, group_count, slots, pick_count,
    tokens, cotangent, routes, probs, rank, gate_hbm, lift_hbm, down_hbm,
    tokens_grad, probs_grad, gate_change, lift_change, down_change,
    meta, line_rows, line_meta, relayed, rows_in, place, hidden_rows, deltas,
    back_out, back_in, sums_gl, sums_down,
    line_out_sem, line_in_sem, near_out_sem, near_in_sem, side_out_sem, side_in_sem,
    relay_out_sem, relay_in_sem, last_out_sem, last_in_sem, back_out_sem, back_in_sem, kernel_sem,
    sums_out_sem, sums_in_sem,
):
    me, group = lax.axis_index("expert"), lax.axis_index("dp")
    token_count, width = tokens.shape
    wide = width // 2
    inner = hidden_rows.shape[1]
    row_count = expert_count * slots
    quarter = width // group_count
    half_gl, half_down = quarter // 2, inner // 2
    piece_gl = half_gl // 2
    chunk_pairs = len(PAIRS) // 4
    chunk_rows = chunk_pairs * CORES * slots
    up, down = (group + 1) % group_count, (group + group_count - 1) % group_count
    across = (group + 2) % group_count
    my_z, my_y, my_core = me // (SIDE * CORES), (me // CORES) % SIDE, me % CORES

    def device(dz, dy, core):
        z, y = (my_z + dz) % SIDE, (my_y + dy) % SIDE
        return (z * SIDE + y) * CORES + (my_core + core) % CORES

    def along(half, offset, core):
        return device(0, offset, core) if half == 0 else device(offset, 0, core)

    def pair_of(half, part, offset):
        offset %= SIDE
        return PAIRS.index((part, offset) if half == 0 else (offset, part))

    barrier = pltpu.get_barrier_semaphore()

    @pl.loop(1, expert_count)
    def _(step):
        pl.semaphore_signal(
            barrier, inc=1, device_id=((me + step) % expert_count, group), device_id_type=MESH
        )

    for neighbour in (up, down):
        pl.semaphore_signal(barrier, inc=1, device_id=(me, neighbour), device_id_type=MESH)

    experts = routes[...]
    hot = experts == rank[0]
    for place_number in range(1, expert_count // 2):
        hot = hot | (experts == rank[place_number])
    facts = jnp.concatenate(
        [
            experts.astype(F32),
            probs[...].astype(F32),
            jnp.where(hot, float(slots), float(slots // 2)),
            jnp.zeros((NOTE - 3 * pick_count, token_count), F32),
        ],
        axis=0,
    )
    meta[...] = facts.T.astype(BF16)

    def remote(source, target, send, receive, expert):
        return pltpu.make_async_remote_copy(
            src_ref=source,
            dst_ref=target,
            send_sem=send,
            recv_sem=receive,
            device_id=(expert, group),
            device_id_type=MESH,
        )

    def line_own(half, way, kind):
        columns = slice(half * wide, (half + 1) * wide)
        source = (tokens.at[:, columns], cotangent.at[:, columns], meta)[kind]
        slot = -STEPS[way] % SIDE - 1
        target = line_meta.at[half, slot] if kind == 2 else line_rows.at[half, slot, kind]
        return remote(
            source, target, line_out_sem.at[half, way, kind], line_in_sem.at[half, slot, kind],
            along(1 - half, STEPS[way], 0),
        )

    def line_on(half, kind):
        way = 1 if kind == 1 else 0
        slot = -STEPS[way] % SIDE - 1
        if kind == 2:
            source, target = line_meta.at[half, slot], line_meta.at[half, 1]
        else:
            source, target = line_rows.at[half, slot, kind], line_rows.at[half, 1, kind]
        return remote(
            source, target, line_out_sem.at[half, 2, kind], line_in_sem.at[half, 1, kind],
            along(1 - half, STEPS[way], 0),
        )

    def near(half, part, way, core, rows_out):
        offset = STEPS[way]
        return remote(
            rows_out.at[half, part, offset, :, core],
            rows_in.at[half, pair_of(half, part, -offset), core],
            near_out_sem.at[half, part, way, core], near_in_sem.at[half, part, way, core],
            along(half, offset, core),
        )

    def beside(half, part, rows_out):
        return remote(
            rows_out.at[half, part, 0, :, 1],
            rows_in.at[half, pair_of(half, part, 0), 1],
            side_out_sem.at[half, part], side_in_sem.at[half, part],
            along(half, 0, 1),
        )

    def relay(half, part, way, rows_out):
        return remote(
            rows_out.at[half, part, 2, way],
            relayed.at[half, way, part],
            relay_out_sem.at[half, part, way], relay_in_sem.at[half, part, way],
            along(half, STEPS[way], 0),
        )

    def last(half, part, way, core):
        return remote(
            relayed.at[half, way, part, core],
            rows_in.at[half, pair_of(half, part, 2), core, way],
            last_out_sem.at[half, part, way, core], last_in_sem.at[half, part, way, core],
            along(half, STEPS[way], core),
        )

    def sends_of(half, part, rows_out):
        return (
            [beside(half, part, rows_out)]
            + [relay(half, part, way, rows_out) for way in range(2)]
            + [near(half, part, way, core, rows_out) for way in range(2) for core in range(CORES)]
        )

    below = jnp.where(
        lax.broadcasted_iota(jnp.int32, (token_count, token_count), 0)
        > lax.broadcasted_iota(jnp.int32, (token_count, token_count), 1),
        1.0,
        0.0,
    ).astype(BF16)
    shift = slots.bit_length() - 1

    def tables(facts, experts):
        lanes = len(experts) * slots
        lane = lax.broadcasted_iota(jnp.int32, (1, lanes), 1)
        block = lax.shift_right_logical(lane, shift)
        slot = lax.bitwise_and(lane, slots - 1).astype(F32)
        named = jnp.zeros((1, lanes), jnp.int32)
        for number, expert in enumerate(experts):
            named = jnp.where(block == number, expert, named)
        named = named.astype(F32)
        facts = facts.astype(F32)
        limit = jnp.zeros((token_count, lanes), F32)
        weight = jnp.zeros((token_count, lanes), F32)
        for pick in range(pick_count):
            hit = facts[:, pick : pick + 1] == named
            weight = jnp.where(hit, facts[:, pick_count + pick : pick_count + pick + 1], weight)
            first = 2 * pick_count + pick
            limit = jnp.where(hit, facts[:, first : first + 1], limit)
        order = dot(below, jnp.where(limit > 0.0, 1.0, 0.0).astype(BF16))
        kept = (order == slot) & (order < limit)
        return (
            jnp.where(kept, 1.0, 0.0).astype(BF16),
            jnp.where(kept, weight, 0.0).astype(BF16),
        )

    def first_part(rows_out, gate, lift, down_kernel):
        loads = [
            pltpu.make_async_copy(source, target, kernel_sem.at[i])
            for i, (source, target) in enumerate(
                ((gate_hbm, gate), (lift_hbm, lift), (down_hbm, down_kernel))
            )
        ]
        for load in loads:
            load.start()
        pl.semaphore_wait(barrier, expert_count + 1)
        for kind in (2, 0, 1):
            for way in range(2):
                for half in range(2):
                    line_own(half, way, kind).start()

        line_experts = [
            [along(half, offset, core) for offset in range(SIDE) for core in range(CORES)]
            for half in range(2)
        ]

        def send_part(part):
            for half in range(2):
                if part == 0:
                    columns = slice(half * wide, (half + 1) * wide)
                    sources = (tokens[:, columns], cotangent[:, columns])
                    facts = meta[...]
                else:
                    sources = (line_rows[half, part - 1, 0], line_rows[half, part - 1, 1])
                    facts = line_meta[half, part - 1]
                for kind, table in enumerate(tables(facts, line_experts[half])):
                    chosen = dot(table, sources[kind], FIRST).astype(BF16)
                    chosen = chosen.reshape(SIDE, CORES, slots, wide)
                    rows_out[half, part, :, kind] = chosen
                    rows_in[half, pair_of(half, part, 0), 0, kind] = chosen[0, 0]
                for copy in sends_of(half, part, rows_out):
                    copy.start()

        def pass_last(part):
            for half in range(2):
                for way in range(2):
                    relay(half, part, way, rows_out).wait_recv()
                    for core in range(CORES):
                        last(half, part, way, core).start()

        send_part(0)
        for half in range(2):
            for kind in (2, 0, 1):
                line_own(half, 0, kind).wait_recv()
                line_own(half, 1, kind).wait_recv()
                line_on(half, kind).start()
        send_part(1)
        send_part(3)
        pass_last(0)
        for half in range(2):
            for kind in range(3):
                line_on(half, kind).wait_recv()
        send_part(2)
        place[...] = tables(
            meta[...], [device(-dz, -dy, core) for dz, dy in PAIRS for core in range(CORES)]
        )[0]
        pass_last(1)
        pass_last(3)
        for load in loads:
            load.wait()

        def await_rows(half, part, offset):
            if offset == 0:
                beside(half, part, rows_out).wait_recv()
            for core in range(CORES):
                if offset == 2:
                    for way in range(2):
                        last(half, part, way, core).wait_recv()
                elif offset:
                    near(half, part, 1 - STEPS.index(offset), core, rows_out).wait_recv()

        @pl.loop(0, len(PAIRS) // chunk_pairs)
        def _(part):
            blocks = pl.ds(part * chunk_pairs, chunk_pairs)
            rows = pl.ds(pl.multiple_of(part * chunk_rows, chunk_rows), chunk_rows)
            for number in range(len(PAIRS) // chunk_pairs):

                @pl.when(part == number)
                def _():
                    if number == 1:
                        pass_last(2)
                    for dz, dy in PAIRS[number * chunk_pairs : (number + 1) * chunk_pairs]:
                        await_rows(0, dz, dy)
                        await_rows(1, dy, dz)

            x, scaled = (
                jnp.concatenate(
                    [rows_in[half, blocks, :, kind].reshape(chunk_rows, wide) for half in range(2)],
                    axis=1,
                )
                for kind in range(2)
            )
            shape = (chunk_pairs * CORES, slots)
            blocks = pl.ds(part * chunk_pairs * CORES, chunk_pairs * CORES)
            gate_pre = dot(x, gate[...])
            lift_pre = dot(x, lift[...])
            sigmoid = jax.nn.sigmoid(gate_pre)
            activated = gate_pre * sigmoid
            hidden = (activated * lift_pre).astype(BF16)
            hidden_rows[rows, :] = hidden
            expert_out = dot(hidden, down_kernel[...])
            prob = jnp.sum(scaled.astype(F32) * expert_out, axis=1, keepdims=True)
            back_out[blocks, :, width:] = (
                jnp.broadcast_to(prob, (chunk_rows, NOTE)).astype(BF16).reshape(*shape, NOTE)
            )
            hidden_delta = dot(scaled, down_kernel[...], LAST)
            lift_delta = (hidden_delta * activated).astype(BF16)
            gate_delta = (
                hidden_delta * lift_pre * sigmoid * (1.0 + gate_pre * (1.0 - sigmoid))
            ).astype(BF16)
            deltas[rows, :inner] = gate_delta
            deltas[rows, inner:] = lift_delta
            route_delta = dot(gate_delta, gate[...], LAST) + dot(lift_delta, lift[...], LAST)
            back_out[blocks, :, :width] = route_delta.astype(BF16).reshape(*shape, width)

        for half in range(2):
            for kind in range(3):
                for way in range(2):
                    line_own(half, way, kind).wait_send()
                line_on(half, kind).wait_send()
            for part in ORDER:
                for copy in sends_of(half, part, rows_out):
                    copy.wait_send()
                for way in range(2):
                    for core in range(CORES):
                        last(half, part, way, core).wait_send()

    kernel_shape = gate_hbm.shape
    pl.run_scoped(
        first_part,
        pltpu.VMEM((2, SIDE, SIDE, 2, CORES, slots, wide), BF16),
        pltpu.VMEM(kernel_shape, BF16),
        pltpu.VMEM(kernel_shape, BF16),
        pltpu.VMEM((inner, width), BF16),
    )

    def give_back(step):
        dz, dy = PAIRS[step // CORES]
        return remote(
            back_out.at[step], back_in.at[step], back_out_sem.at[step], back_in_sem.at[step],
            device(dz, dy, step % CORES),
        )

    fraction = wide // quarter

    def term(part, half, piece):
        first = (part % fraction) * quarter
        if piece == 2:
            columns = pl.ds(pl.multiple_of(first, quarter), quarter)
            scaled = rows_in[part // fraction, :, :, 1, :, columns].reshape(row_count, quarter)
            return dot(hidden_rows[:, half * half_down : (half + 1) * half_down], scaled, FIRST)
        first += half * half_gl + piece * piece_gl
        columns = pl.ds(pl.multiple_of(first, piece_gl), piece_gl)
        x = rows_in[part // fraction, :, :, 0, :, columns].reshape(row_count, piece_gl)
        return dot(x, deltas[...], FIRST)

    def second_part(partial_gl, partial_down):
        plan = (
            (across, 0, down, None),
            (across, 1, up, None),
            (up, 0, up, None),
            (down, 1, down, None),
            (down, 0, down, 0),
            (up, 1, up, 1),
        )

        def view(gl, in_down, number, piece):
            if piece == 2:
                return in_down.at[number]
            return gl.at[number, piece * piece_gl : (piece + 1) * piece_gl]

        def pass_on(number, piece):
            return pltpu.make_async_remote_copy(
                src_ref=view(partial_gl, partial_down, number, piece),
                dst_ref=view(sums_gl, sums_down, number, piece),
                send_sem=sums_out_sem.at[number, piece],
                recv_sem=sums_in_sem.at[number, piece],
                device_id=(me, plan[number][2]),
                device_id_type=MESH,
            )

        def send_sums(numbers):
            for piece in range(3):
                for number in numbers:
                    part, half, _, taken = plan[number]
                    value = term(part, half, piece)
                    if taken is not None:
                        pass_on(taken, piece).wait_recv()
                        value = value + view(sums_gl, sums_down, taken, piece)[...].astype(F32)
                    view(partial_gl, partial_down, number, piece)[...] = value.astype(BF16)
                    pass_on(number, piece).start()

        def keep(half, piece, value, more):
            if piece == 2:
                rows = slice(half * half_down, (half + 1) * half_down)
                targets = ((down_change, value),)
            else:
                rows = slice(half * half_gl + piece * piece_gl, half * half_gl + (piece + 1) * piece_gl)
                targets = ((gate_change, value[:, :inner]), (lift_change, value[:, inner:]))
            for target, values in targets:
                target[0, rows, :] = target[0, rows, :] + values if more else values

        def take(number, half, piece):
            pass_on(number, piece).wait_recv()
            value = view(sums_gl, sums_down, number, piece)[...].astype(F32)
            keep(half, piece, value, True)

        send_sums((0, 1))
        for step in range(1, expert_count):
            give_back(step).start()
        send_sums((2, 3))
        for piece in range(3):
            for half in range(2):
                keep(half, piece, term(group, half, piece), False)
        send_sums((4, 5))

        back_in[0] = back_out[0]

        for step in range(1, expert_count):
            give_back(step).wait_recv()

        returned = back_in[:, :, :width].reshape(row_count, width)
        tokens_grad[...] = dot(place[...], returned).astype(BF16)
        notes = back_in[:, :, width:].reshape(row_count, NOTE)
        note_row = lax.broadcasted_iota(jnp.int32, (row_count, NOTE), 0)
        note_lane = lax.broadcasted_iota(jnp.int32, (row_count, NOTE), 1)
        note_step = lax.shift_right_logical(note_row, slots.bit_length() - 1)
        notes = jnp.where(note_step == note_lane, notes.astype(F32), 0.0).astype(BF16)
        by_step = dot(place[...], notes)
        note_lane = lax.broadcasted_iota(jnp.int32, (1, NOTE), 1)
        sender = jnp.full((1, NOTE), -1, jnp.int32)
        for number in range(expert_count):
            dz, dy = PAIRS[number // CORES]
            sender = jnp.where(note_lane == number, device(-dz, -dy, number % CORES), sender)
        sender = sender.astype(F32)
        facts = meta[...].astype(F32)
        pick_lane = lax.broadcasted_iota(jnp.int32, (token_count, pick_count), 1)
        total = jnp.zeros((token_count, pick_count), F32)
        for pick in range(pick_count):
            value = jnp.where(facts[:, pick : pick + 1] == sender, by_step, 0.0)
            value = jnp.sum(value, axis=1, keepdims=True)
            total = jnp.where(pick_lane == pick, value, total)
        total = jnp.concatenate([total, jnp.zeros((token_count, NOTE - pick_count), F32)], axis=1)
        probs_grad[...] = (total.T[:pick_count] / probs[...].astype(F32)).astype(BF16)

        for numbers in ((2, 3), (4, 5)):
            for piece in range(3):
                for half, number in enumerate(numbers):
                    take(number, half, piece)
        for number in range(len(plan)):
            for piece in range(3):
                pass_on(number, piece).wait_send()

        for step in range(1, expert_count):
            give_back(step).wait_send()

    pl.run_scoped(
        second_part,
        pltpu.VMEM((6, half_gl, 2 * inner), BF16),
        pltpu.VMEM((6, half_down, quarter), BF16),
    )


def shards(
    tokens, cotangent, route_ids, gate_probs, expert_rank, gate_kernel, lift_kernel, down_kernel
):
    expert_count = lax.axis_size("expert")
    group_count = lax.axis_size("dp")
    token_count, pick_count = route_ids.shape
    width = tokens.shape[1]
    inner = gate_kernel.shape[2]
    slots = token_count * pick_count // expert_count
    row_count = expert_count * slots
    quarter = width // group_count
    vmem, anywhere = pl.BlockSpec(memory_space=pltpu.VMEM), pl.BlockSpec(memory_space=pl.ANY)
    dma = pltpu.SemaphoreType.DMA
    outputs = pl.pallas_call(
        functools.partial(layer_kernel, expert_count, group_count, slots, pick_count),
        out_shape=(
            pltpu.VMEM(tokens.shape, BF16),
            pltpu.VMEM((pick_count, token_count), BF16),
            pltpu.VMEM((1, quarter, inner), F32),
            pltpu.VMEM((1, quarter, inner), F32),
            pltpu.VMEM((1, inner, quarter), F32),
        ),
        in_specs=[vmem] * 4 + [pl.BlockSpec(memory_space=pltpu.SMEM)] + [anywhere] * 3,
        out_specs=[vmem] * 5,
        scratch_shapes=[
            pltpu.VMEM((token_count, NOTE), BF16),
            pltpu.VMEM((2, SIDE - 1, 2, token_count, width // 2), BF16),
            pltpu.VMEM((2, SIDE - 1, token_count, NOTE), BF16),
            pltpu.VMEM((2, 2, SIDE, CORES, slots, width // 2), BF16),
            pltpu.VMEM((2, len(PAIRS), CORES, 2, slots, width // 2), BF16),
            pltpu.VMEM((token_count, row_count), BF16),
            pltpu.VMEM((row_count, inner), BF16),
            pltpu.VMEM((row_count, 2 * inner), BF16),
            pltpu.VMEM((expert_count, slots, width + NOTE), BF16),
            pltpu.VMEM((expert_count, slots, width + NOTE), BF16),
            pltpu.VMEM((6, quarter // 2, 2 * inner), BF16),
            pltpu.VMEM((6, inner // 2, quarter), BF16),
            dma((2, 3, 3)),
            dma((2, 3, 3)),
            dma((2, SIDE, 2, CORES)),
            dma((2, SIDE, 2, CORES)),
            dma((2, SIDE)),
            dma((2, SIDE)),
            dma((2, SIDE, 2)),
            dma((2, SIDE, 2)),
            dma((2, SIDE, 2, CORES)),
            dma((2, SIDE, 2, CORES)),
            dma((expert_count,)),
            dma((expert_count,)),
            dma((3,)),
            dma((6, 3)),
            dma((6, 3)),
        ],
        compiler_params=pltpu.CompilerParams(
            collective_id=0, has_side_effects=True, vmem_limit_bytes=58 * 1024 * 1024
        ),
        cost_estimate=pl.CostEstimate(
            flops=18 * row_count * width * inner,
            bytes_accessed=16 * 1024 * 1024,
            transcendentals=row_count * inner,
        ),
    )(
        tokens, cotangent, route_ids.T, gate_probs.T, expert_rank,
        gate_kernel[0], lift_kernel[0], down_kernel[0],
    )
    return (outputs[0], outputs[1].T, *outputs[2:])


def solution(mesh):
    return jax.shard_map(
        shards,
        mesh=mesh,
        in_specs=(
            P(("expert", "dp"), None),
            P(("expert", "dp"), None),
            P(("expert", "dp"), None),
            P(("expert", "dp"), None),
            P(),
            P("expert", None, None),
            P("expert", None, None),
            P("expert", None, None),
        ),
        out_specs=(
            P(("expert", "dp"), None),
            P(("expert", "dp"), None),
            P("expert", "dp", None),
            P("expert", "dp", None),
            P("expert", None, "dp"),
        ),
        check_vma=False,
    )
```

```python
import functools

import jax
import jax.numpy as jnp
from jax import lax
from jax.experimental import pallas as pl
from jax.experimental.pallas import tpu as pltpu
from jax.sharding import PartitionSpec as P

MESH = pl.DeviceIdType.MESH
FACTS = 32
NOTE = 128
FIRST = (((0,), (0,)), ((), ()))
LAST = (((1,), (1,)), ((), ()))
F32 = jnp.float32
BF16 = jnp.bfloat16


def dot(a, b, dims=(((1,), (0,)), ((), ()))):
    return lax.dot_general(a, b, dims, preferred_element_type=F32)


ORDER = (0, 1, 3, 2)
PAIRS = tuple(
    sorted(
        ((dz, dy) for dz in ORDER for dy in ORDER),
        key=lambda pair: sorted((ORDER.index(pair[0]), ORDER.index(pair[1])), reverse=True),
    )
)
SIDE = 4
CORES = 2
STEPS = (1, 3)


def layer_kernel(
    expert_count, group_count, slots, pick_count,
    tokens, cotangent, routes, probs, rank, gate_hbm, lift_hbm, down_hbm,
    tokens_grad, probs_grad, gate_change, lift_change, down_change,
    meta, line_rows, line_meta, relayed, rows_in, place, hidden_rows, deltas,
    gate, lift, down_kernel,
    back_out, back_in, sums_gl, sums_down,
    line_out_sem, line_in_sem, near_out_sem, near_in_sem, side_out_sem, side_in_sem,
    relay_out_sem, relay_in_sem, last_out_sem, last_in_sem, back_out_sem, back_in_sem, kernel_sem,
    sums_out_sem, sums_in_sem,
):
    me, group = lax.axis_index("expert"), lax.axis_index("dp")
    token_count, width = tokens.shape
    wide = width // 2
    inner = hidden_rows.shape[1]
    row_count = expert_count * slots
    quarter = width // group_count
    half_gl, half_down = quarter // 2, inner // 2
    piece_gl = half_gl // 2
    chunk_pairs = len(PAIRS) // 4
    chunk_rows = chunk_pairs * CORES * slots
    chunks = len(PAIRS) // chunk_pairs
    up, down = (group + 1) % group_count, (group + group_count - 1) % group_count
    across = (group + 2) % group_count
    my_z, my_y, my_core = me // (SIDE * CORES), (me // CORES) % SIDE, me % CORES

    def device(dz, dy, core):
        z, y = (my_z + dz) % SIDE, (my_y + dy) % SIDE
        return (z * SIDE + y) * CORES + (my_core + core) % CORES

    def along(half, offset, core):
        return device(0, offset, core) if half == 0 else device(offset, 0, core)

    def pair_of(half, part, offset):
        offset %= SIDE
        return PAIRS.index((part, offset) if half == 0 else (offset, part))

    barrier = pltpu.get_barrier_semaphore()

    neighbours = [(along(half, offset, core), group)
                  for half in range(2) for offset in STEPS for core in range(CORES)]
    neighbours += [(device(0, 0, 1), group), (me, up), (me, down)]
    for neighbour in neighbours:
        pl.semaphore_signal(barrier, inc=1, device_id=neighbour, device_id_type=MESH)

    experts = routes[...]
    hot = experts == rank[0]
    for place_number in range(1, expert_count // 2):
        hot = hot | (experts == rank[place_number])
    facts = jnp.concatenate(
        [
            experts.astype(F32),
            probs[...].astype(F32),
            jnp.where(hot, float(slots), float(slots // 2)),
            jnp.zeros((FACTS - 3 * pick_count, token_count), F32),
        ],
        axis=0,
    )
    meta[...] = facts.astype(BF16)

    def remote(source, target, send, receive, expert):
        return pltpu.make_async_remote_copy(
            src_ref=source,
            dst_ref=target,
            send_sem=send,
            recv_sem=receive,
            device_id=(expert, group),
            device_id_type=MESH,
        )

    def line_own(half, way, kind):
        columns = slice(half * wide, (half + 1) * wide)
        source = (tokens.at[:, columns], cotangent.at[:, columns], meta)[kind]
        slot = -STEPS[way] % SIDE - 1
        target = line_meta.at[half, slot] if kind == 2 else line_rows.at[half, slot, kind]
        return remote(
            source, target, line_out_sem.at[half, way, kind], line_in_sem.at[half, slot, kind],
            along(1 - half, STEPS[way], 0),
        )

    def line_on(half, kind):
        way = 1 if kind == 1 else 0
        slot = -STEPS[way] % SIDE - 1
        if kind == 2:
            source, target = line_meta.at[half, slot], line_meta.at[half, 1]
        else:
            source, target = line_rows.at[half, slot, kind], line_rows.at[half, 1, kind]
        return remote(
            source, target, line_out_sem.at[half, 2, kind], line_in_sem.at[half, 1, kind],
            along(1 - half, STEPS[way], 0),
        )

    def near(half, part, way, core, rows_out):
        offset = STEPS[way]
        return remote(
            rows_out.at[half, part, offset, :, core],
            rows_in.at[half, pair_of(half, part, -offset), core],
            near_out_sem.at[half, part, way, core], near_in_sem.at[half, part, way, core],
            along(half, offset, core),
        )

    def beside(half, part, rows_out):
        return remote(
            rows_out.at[half, part, 0, :, 1],
            rows_in.at[half, pair_of(half, part, 0), 1],
            side_out_sem.at[half, part], side_in_sem.at[half, part],
            along(half, 0, 1),
        )

    def relay(half, part, way, rows_out):
        return remote(
            rows_out.at[half, part, 2, way],
            relayed.at[half, way, part],
            relay_out_sem.at[half, part, way], relay_in_sem.at[half, part, way],
            along(half, STEPS[way], 0),
        )

    def last(half, part, way, core):
        return remote(
            relayed.at[half, way, part, core],
            rows_in.at[half, pair_of(half, part, 2), core, way],
            last_out_sem.at[half, part, way, core], last_in_sem.at[half, part, way, core],
            along(half, STEPS[way], core),
        )

    def relays_of(half, part, rows_out):
        return [relay(half, part, way, rows_out) for way in range(2)]

    def direct_of(half, part, rows_out):
        return [beside(half, part, rows_out)] + [
            near(half, part, way, core, rows_out) for way in range(2) for core in range(CORES)
        ]

    below = jnp.where(
        lax.broadcasted_iota(jnp.int32, (token_count, token_count), 0)
        > lax.broadcasted_iota(jnp.int32, (token_count, token_count), 1),
        1.0,
        0.0,
    ).astype(BF16)
    shift = slots.bit_length() - 1

    def tables(facts, experts):
        lanes = len(experts) * slots
        lane = lax.broadcasted_iota(jnp.int32, (1, lanes), 1)
        block = lax.shift_right_logical(lane, shift)
        slot = lax.bitwise_and(lane, slots - 1).astype(F32)
        named = jnp.zeros((1, lanes), jnp.int32)
        for number, expert in enumerate(experts):
            named = jnp.where(block == number, expert, named)
        named = named.astype(F32)
        facts = facts.astype(F32).T
        limit = jnp.zeros((token_count, lanes), F32)
        weight = jnp.zeros((token_count, lanes), F32)
        for pick in range(pick_count):
            hit = facts[:, pick : pick + 1] == named
            weight = jnp.where(hit, facts[:, pick_count + pick : pick_count + pick + 1], weight)
            first = 2 * pick_count + pick
            limit = jnp.where(hit, facts[:, first : first + 1], limit)
        order = dot(below, jnp.where(limit > 0.0, 1.0, 0.0).astype(BF16))
        kept = (order == slot) & (order < limit)
        return (
            jnp.where(kept, 1.0, 0.0).astype(BF16),
            jnp.where(kept, weight, 0.0).astype(BF16),
        )

    def chunk_of(part, kind):
        blocks = pl.ds(part * chunk_pairs, chunk_pairs)
        halves = [rows_in[half, blocks, :, kind].reshape(chunk_rows, wide) for half in range(2)]
        return jnp.concatenate(halves, axis=1)

    def first_half(part):
        rows = pl.ds(pl.multiple_of(part * chunk_rows, chunk_rows), chunk_rows)
        x = chunk_of(part, 0)
        gate_pre = dot(x, gate[...])
        lift_pre = dot(x, lift[...])
        sigmoid = jax.nn.sigmoid(gate_pre)
        activated = gate_pre * sigmoid
        hidden_rows[rows, :] = (activated * lift_pre).astype(BF16)
        hidden_delta = dot(chunk_of(part, 1), down_kernel[...], LAST)
        deltas[rows, :inner] = (
            hidden_delta * lift_pre * sigmoid * (1.0 + gate_pre * (1.0 - sigmoid))
        ).astype(BF16)
        deltas[rows, inner:] = (hidden_delta * activated).astype(BF16)

    def second_half(part):
        rows = pl.ds(pl.multiple_of(part * chunk_rows, chunk_rows), chunk_rows)
        blocks = pl.ds(part * chunk_pairs * CORES, chunk_pairs * CORES)
        shape = (chunk_pairs * CORES, slots)
        expert_out = dot(hidden_rows[rows, :], down_kernel[...])
        prob = jnp.sum(chunk_of(part, 1).astype(F32) * expert_out, axis=1, keepdims=True)
        prob = jnp.broadcast_to(prob, (chunk_rows, NOTE)).astype(BF16)
        back_out[blocks, :, width:] = prob.reshape(*shape, NOTE)
        route_delta = dot(deltas[rows, :inner], gate[...], LAST)
        route_delta = route_delta + dot(deltas[rows, inner:], lift[...], LAST)
        back_out[blocks, :, :width] = route_delta.astype(BF16).reshape(*shape, width)

    def first_part(rows_out):
        loads = [
            pltpu.make_async_copy(source, target, kernel_sem.at[i])
            for i, (source, target) in enumerate(
                ((gate_hbm, gate), (lift_hbm, lift), (down_hbm, down_kernel))
            )
        ]
        for load in loads:
            load.start()
        pl.semaphore_wait(barrier, len(neighbours))
        for kind in (2, 0, 1):
            for way in range(2):
                for half in range(2):
                    line_own(half, way, kind).start()

        line_experts = [
            [along(half, offset, core) for offset in range(SIDE) for core in range(CORES)]
            for half in range(2)
        ]

        def choose(part):
            for half in range(2):
                if part == 0:
                    columns = slice(half * wide, (half + 1) * wide)
                    sources = (tokens[:, columns], cotangent[:, columns])
                    known = meta[...]
                else:
                    sources = (line_rows[half, part - 1, 0], line_rows[half, part - 1, 1])
                    known = line_meta[half, part - 1]
                for kind, table in enumerate(tables(known, line_experts[half])):
                    chosen = dot(table, sources[kind], FIRST).astype(BF16)
                    chosen = chosen.reshape(SIDE, CORES, slots, wide)
                    rows_out[half, part, :, kind] = chosen
                    rows_in[half, pair_of(half, part, 0), 0, kind] = chosen[0, 0]

        def send(part, copies_of):
            for half in range(2):
                for copy in copies_of(half, part, rows_out):
                    copy.start()

        def pass_last(part):
            for half in range(2):
                for way in range(2):
                    relay(half, part, way, rows_out).wait_recv()
                    for core in range(CORES):
                        last(half, part, way, core).start()

        choose(0)
        for half in range(2):
            for kind in (2, 0, 1):
                line_own(half, 0, kind).wait_recv()
                line_own(half, 1, kind).wait_recv()
                line_on(half, kind).start()
        send(0, relays_of)
        send(0, direct_of)
        choose(1)
        send(1, relays_of)
        send(1, direct_of)
        choose(3)
        send(3, relays_of)
        pass_last(0)
        for half in range(2):
            for kind in range(3):
                line_on(half, kind).wait_recv()
        choose(2)
        send(2, relays_of)
        send(3, direct_of)
        send(2, direct_of)
        place[...] = tables(
            meta[...], [device(-dz, -dy, core) for dz, dy in PAIRS for core in range(CORES)]
        )[0]
        pass_last(1)
        for load in loads:
            load.wait()

        def await_rows(half, part, offset):
            if offset == 0:
                beside(half, part, rows_out).wait_recv()
            for core in range(CORES):
                if offset == 2:
                    for way in range(2):
                        last(half, part, way, core).wait_recv()
                elif offset:
                    near(half, part, 1 - STEPS.index(offset), core, rows_out).wait_recv()

        @pl.loop(0, chunks)
        def _(part):
            for number in range(chunks):

                @pl.when(part == number)
                def _():
                    if number == 1:
                        pass_last(3)
                        pass_last(2)
                    for dz, dy in PAIRS[number * chunk_pairs : (number + 1) * chunk_pairs]:
                        await_rows(0, dz, dy)
                        await_rows(1, dy, dz)

            first_half(part)

            @pl.when(part < chunks - 1)
            def _():
                second_half(part)

        for half in range(2):
            for kind in range(3):
                for way in range(2):
                    line_own(half, way, kind).wait_send()
                line_on(half, kind).wait_send()
            for part in ORDER:
                for copy in relays_of(half, part, rows_out) + direct_of(half, part, rows_out):
                    copy.wait_send()
                for way in range(2):
                    for core in range(CORES):
                        last(half, part, way, core).wait_send()

    pl.run_scoped(first_part, pltpu.VMEM((2, SIDE, SIDE, 2, CORES, slots, wide), BF16))

    def give_back(step):
        dz, dy = PAIRS[step // CORES]
        return remote(
            back_out.at[step], back_in.at[step], back_out_sem.at[step], back_in_sem.at[step],
            device(dz, dy, step % CORES),
        )

    fraction = wide // quarter

    def term(part, half, piece):
        first = (part % fraction) * quarter
        if piece == 2:
            columns = pl.ds(pl.multiple_of(first, quarter), quarter)
            scaled = rows_in[part // fraction, :, :, 1, :, columns].reshape(row_count, quarter)
            return dot(hidden_rows[:, half * half_down : (half + 1) * half_down], scaled, FIRST)
        first += half * half_gl + piece * piece_gl
        columns = pl.ds(pl.multiple_of(first, piece_gl), piece_gl)
        x = rows_in[part // fraction, :, :, 0, :, columns].reshape(row_count, piece_gl)
        return dot(x, deltas[...], FIRST)

    def second_part(partial_gl, partial_down):
        plan = (
            (across, 0, down, None),
            (across, 1, up, None),
            (up, 0, up, None),
            (down, 1, down, None),
            (down, 0, down, 0),
            (up, 1, up, 1),
        )

        def view(gl, in_down, number, piece):
            if piece == 2:
                return in_down.at[number]
            return gl.at[number, piece * piece_gl : (piece + 1) * piece_gl]

        def pass_on(number, piece):
            return pltpu.make_async_remote_copy(
                src_ref=view(partial_gl, partial_down, number, piece),
                dst_ref=view(sums_gl, sums_down, number, piece),
                send_sem=sums_out_sem.at[number, piece],
                recv_sem=sums_in_sem.at[number, piece],
                device_id=(me, plan[number][2]),
                device_id_type=MESH,
            )

        def send_sums(numbers, before=(None, None)):
            for piece in range(3):
                for number, earlier in zip(numbers, before):
                    part, half, _, taken = plan[number]
                    value = term(part, half, piece)
                    if taken is not None:
                        pass_on(taken, piece).wait_recv()
                        value = value + view(sums_gl, sums_down, taken, piece)[...].astype(F32)
                    view(partial_gl, partial_down, number, piece)[...] = value.astype(BF16)
                    if earlier is not None:
                        pass_on(earlier, piece).wait_send()
                    pass_on(number, piece).start()

        def keep(half, piece, value, more):
            if piece == 2:
                rows = slice(half * half_down, (half + 1) * half_down)
                targets = ((down_change, value),)
            else:
                rows = slice(half * half_gl + piece * piece_gl, half * half_gl + (piece + 1) * piece_gl)
                targets = ((gate_change, value[:, :inner]), (lift_change, value[:, inner:]))
            for target, values in targets:
                target[0, rows, :] = target[0, rows, :] + values if more else values

        def take(number, half, piece):
            pass_on(number, piece).wait_recv()
            value = view(sums_gl, sums_down, number, piece)[...].astype(F32)
            keep(half, piece, value, True)

        send_sums((0, 1))
        second_half(chunks - 1)
        for step in range(1, expert_count):
            give_back(step).start()
        send_sums((3, 2), (0, 1))
        for piece in range(3):
            for half in range(2):
                keep(half, piece, term(group, half, piece), False)
        send_sums((4, 5), (3, 2))

        back_in[0] = back_out[0]

        for step in range(1, expert_count):
            give_back(step).wait_recv()

        returned = back_in[:, :, :width].reshape(row_count, width)
        tokens_grad[...] = dot(place[...], returned).astype(BF16)
        notes = back_in[:, :, width:].reshape(row_count, NOTE)
        note_row = lax.broadcasted_iota(jnp.int32, (row_count, NOTE), 0)
        note_lane = lax.broadcasted_iota(jnp.int32, (row_count, NOTE), 1)
        note_step = lax.shift_right_logical(note_row, slots.bit_length() - 1)
        notes = jnp.where(note_step == note_lane, notes.astype(F32), 0.0).astype(BF16)
        by_step = dot(place[...], notes)
        note_lane = lax.broadcasted_iota(jnp.int32, (1, NOTE), 1)
        sender = jnp.full((1, NOTE), -1, jnp.int32)
        for number in range(expert_count):
            dz, dy = PAIRS[number // CORES]
            sender = jnp.where(note_lane == number, device(-dz, -dy, number % CORES), sender)
        sender = sender.astype(F32)
        facts = meta[...].astype(F32).T
        pick_lane = lax.broadcasted_iota(jnp.int32, (token_count, pick_count), 1)
        total = jnp.zeros((token_count, pick_count), F32)
        for pick in range(pick_count):
            value = jnp.where(facts[:, pick : pick + 1] == sender, by_step, 0.0)
            value = jnp.sum(value, axis=1, keepdims=True)
            total = jnp.where(pick_lane == pick, value, total)
        total = jnp.concatenate([total, jnp.zeros((token_count, NOTE - pick_count), F32)], axis=1)
        probs_grad[...] = (total.T[:pick_count] / probs[...].astype(F32)).astype(BF16)

        for numbers in ((2, 3), (4, 5)):
            for piece in range(3):
                for half, number in enumerate(numbers):
                    take(number, half, piece)
        for number in (4, 5):
            for piece in range(3):
                pass_on(number, piece).wait_send()

        for step in range(1, expert_count):
            give_back(step).wait_send()

    pl.run_scoped(
        second_part,
        pltpu.VMEM((6, half_gl, 2 * inner), BF16),
        pltpu.VMEM((6, half_down, quarter), BF16),
    )


def finish_kernel(*refs):
    count = (len(refs) - 1) // 2
    copies = [
        pltpu.make_async_copy(refs[i], refs[count + i], refs[-1].at[i]) for i in range(count)
    ]
    for copy in copies:
        copy.start()
    for copy in copies:
        copy.wait()


def shards(
    tokens, cotangent, route_ids, gate_probs, expert_rank, gate_kernel, lift_kernel, down_kernel
):
    expert_count = lax.axis_size("expert")
    group_count = lax.axis_size("dp")
    token_count, pick_count = route_ids.shape
    width = tokens.shape[1]
    inner = gate_kernel.shape[2]
    slots = token_count * pick_count // expert_count
    row_count = expert_count * slots
    quarter = width // group_count
    vmem, anywhere = pl.BlockSpec(memory_space=pltpu.VMEM), pl.BlockSpec(memory_space=pl.ANY)
    dma = pltpu.SemaphoreType.DMA
    outputs = pl.pallas_call(
        functools.partial(layer_kernel, expert_count, group_count, slots, pick_count),
        out_shape=(
            pltpu.VMEM(tokens.shape, BF16),
            pltpu.VMEM((pick_count, token_count), BF16),
            pltpu.VMEM((1, quarter, inner), F32),
            pltpu.VMEM((1, quarter, inner), F32),
            pltpu.VMEM((1, inner, quarter), F32),
        ),
        in_specs=[vmem] * 4 + [pl.BlockSpec(memory_space=pltpu.SMEM)] + [anywhere] * 3,
        out_specs=[vmem] * 5,
        scratch_shapes=[
            pltpu.VMEM((FACTS, token_count), BF16),
            pltpu.VMEM((2, SIDE - 1, 2, token_count, width // 2), BF16),
            pltpu.VMEM((2, SIDE - 1, FACTS, token_count), BF16),
            pltpu.VMEM((2, 2, SIDE, CORES, slots, width // 2), BF16),
            pltpu.VMEM((2, len(PAIRS), CORES, 2, slots, width // 2), BF16),
            pltpu.VMEM((token_count, row_count), BF16),
            pltpu.VMEM((row_count, inner), BF16),
            pltpu.VMEM((row_count, 2 * inner), BF16),
            pltpu.VMEM((width, inner), BF16),
            pltpu.VMEM((width, inner), BF16),
            pltpu.VMEM((inner, width), BF16),
            pltpu.VMEM((expert_count, slots, width + NOTE), BF16),
            pltpu.VMEM((expert_count, slots, width + NOTE), BF16),
            pltpu.VMEM((6, quarter // 2, 2 * inner), BF16),
            pltpu.VMEM((6, inner // 2, quarter), BF16),
            dma((2, 3, 3)),
            dma((2, 3, 3)),
            dma((2, SIDE, 2, CORES)),
            dma((2, SIDE, 2, CORES)),
            dma((2, SIDE)),
            dma((2, SIDE)),
            dma((2, SIDE, 2)),
            dma((2, SIDE, 2)),
            dma((2, SIDE, 2, CORES)),
            dma((2, SIDE, 2, CORES)),
            dma((expert_count,)),
            dma((expert_count,)),
            dma((3,)),
            dma((6, 3)),
            dma((6, 3)),
        ],
        compiler_params=pltpu.CompilerParams(
            collective_id=0, has_side_effects=True, vmem_limit_bytes=58 * 1024 * 1024
        ),
        cost_estimate=pl.CostEstimate(
            flops=18 * row_count * width * inner,
            bytes_accessed=16 * 1024 * 1024,
            transcendentals=row_count * inner,
        ),
    )(
        tokens, cotangent, route_ids.T, gate_probs.T, expert_rank,
        gate_kernel[0], lift_kernel[0], down_kernel[0],
    )
    outputs = pl.pallas_call(
        finish_kernel,
        out_shape=[jax.ShapeDtypeStruct(item.shape, item.dtype) for item in outputs],
        in_specs=[vmem] * 5,
        out_specs=[anywhere] * 5,
        scratch_shapes=[dma((5,))],
    )(*outputs)
    return (outputs[0], outputs[1].T, *outputs[2:])


def solution(mesh):
    return jax.shard_map(
        shards,
        mesh=mesh,
        in_specs=(
            P(("expert", "dp"), None),
            P(("expert", "dp"), None),
            P(("expert", "dp"), None),
            P(("expert", "dp"), None),
            P(),
            P("expert", None, None),
            P("expert", None, None),
            P("expert", None, None),
        ),
        out_specs=(
            P(("expert", "dp"), None),
            P(("expert", "dp"), None),
            P("expert", "dp", None),
            P("expert", "dp", None),
            P("expert", None, "dp"),
        ),
        check_vma=False,
    )
```

```python
import functools

import jax
import jax.numpy as jnp
from jax import lax
from jax.experimental import pallas as pl
from jax.experimental.pallas import tpu as pltpu
from jax.sharding import PartitionSpec as P

MESH = pl.DeviceIdType.MESH
FACTS = 32
NOTE = 128
FIRST = (((0,), (0,)), ((), ()))
LAST = (((1,), (1,)), ((), ()))
F32 = jnp.float32
BF16 = jnp.bfloat16


def dot(a, b, dims=(((1,), (0,)), ((), ()))):
    return lax.dot_general(a, b, dims, preferred_element_type=F32)


ORDER = (0, 1, 3, 2)
PAIRS = tuple(
    sorted(
        ((dz, dy) for dz in ORDER for dy in ORDER),
        key=lambda pair: sorted((ORDER.index(pair[0]), ORDER.index(pair[1])), reverse=True),
    )
)
CORES = 2
BACK = (1,) + tuple(
    PAIRS.index(pair) * CORES + core
    for pairs in (
        ((0, 1), (1, 0), (0, 3), (3, 0)),
        ((1, 1), (1, 3), (3, 1)),
        ((3, 3), (0, 2), (2, 0)),
        ((2, 1), (1, 2), (2, 3), (3, 2)),
        ((2, 2),),
    )
    for core in range(CORES)
    for pair in pairs
)
SIDE = 4
STEPS = (1, 3)


def layer_kernel(
    expert_count, group_count, slots, pick_count,
    tokens, cotangent, routes, probs, rank, gate_hbm, lift_hbm, down_hbm,
    tokens_grad, probs_grad, gate_change, lift_change, down_change,
    meta, line_rows, line_meta, relayed, rows_in, place, hidden_rows, deltas,
    gate, lift, down_kernel,
    back_out, back_in, sums_gl, sums_down,
    line_out_sem, line_in_sem, near_out_sem, near_in_sem, side_out_sem, side_in_sem,
    relay_out_sem, relay_in_sem, last_out_sem, last_in_sem, back_out_sem, back_in_sem, kernel_sem,
    sums_out_sem, sums_in_sem,
):
    me, group = lax.axis_index("expert"), lax.axis_index("dp")
    token_count, width = tokens.shape
    wide = width // 2
    inner = hidden_rows.shape[1]
    row_count = expert_count * slots
    quarter = width // group_count
    half_gl, half_down = quarter // 2, inner // 2
    piece_gl = half_gl // 2
    chunk_pairs = len(PAIRS) // 4
    chunk_rows = chunk_pairs * CORES * slots
    chunks = len(PAIRS) // chunk_pairs
    up, down = (group + 1) % group_count, (group + group_count - 1) % group_count
    across = (group + 2) % group_count
    my_z, my_y, my_core = me // (SIDE * CORES), (me // CORES) % SIDE, me % CORES

    def device(dz, dy, core):
        z, y = (my_z + dz) % SIDE, (my_y + dy) % SIDE
        return (z * SIDE + y) * CORES + (my_core + core) % CORES

    def along(half, offset, core):
        return device(0, offset, core) if half == 0 else device(offset, 0, core)

    def pair_of(half, part, offset):
        offset %= SIDE
        return PAIRS.index((part, offset) if half == 0 else (offset, part))

    barrier = pltpu.get_barrier_semaphore()

    neighbours = [(along(half, offset, core), group)
                  for half in range(2) for offset in STEPS for core in range(CORES)]
    neighbours += [(device(0, 0, 1), group), (me, up), (me, down)]
    for neighbour in neighbours:
        pl.semaphore_signal(barrier, inc=1, device_id=neighbour, device_id_type=MESH)

    experts = routes[...]
    hot = experts == rank[0]
    for place_number in range(1, expert_count // 2):
        hot = hot | (experts == rank[place_number])
    facts = jnp.concatenate(
        [
            experts.astype(F32),
            probs[...].astype(F32),
            jnp.where(hot, float(slots), float(slots // 2)),
            jnp.zeros((FACTS - 3 * pick_count, token_count), F32),
        ],
        axis=0,
    )
    meta[...] = facts.astype(BF16)

    def remote(source, target, send, receive, expert):
        return pltpu.make_async_remote_copy(
            src_ref=source,
            dst_ref=target,
            send_sem=send,
            recv_sem=receive,
            device_id=(expert, group),
            device_id_type=MESH,
        )

    def line_own(half, way, kind):
        columns = slice(half * wide, (half + 1) * wide)
        source = (tokens.at[:, columns], cotangent.at[:, columns], meta)[kind]
        slot = -STEPS[way] % SIDE - 1
        target = line_meta.at[half, slot] if kind == 2 else line_rows.at[half, slot, kind]
        return remote(
            source, target, line_out_sem.at[half, way, kind], line_in_sem.at[half, slot, kind],
            along(1 - half, STEPS[way], 0),
        )

    def line_on(half, kind):
        way = 1 if kind == 1 else 0
        slot = -STEPS[way] % SIDE - 1
        if kind == 2:
            source, target = line_meta.at[half, slot], line_meta.at[half, 1]
        else:
            source, target = line_rows.at[half, slot, kind], line_rows.at[half, 1, kind]
        return remote(
            source, target, line_out_sem.at[half, 2, kind], line_in_sem.at[half, 1, kind],
            along(1 - half, STEPS[way], 0),
        )

    def near(half, part, way, core, rows_out):
        offset = STEPS[way]
        return remote(
            rows_out.at[half, part, offset, :, core],
            rows_in.at[half, pair_of(half, part, -offset), core],
            near_out_sem.at[half, part, way, core], near_in_sem.at[half, part, way, core],
            along(half, offset, core),
        )

    def beside(half, part, rows_out):
        return remote(
            rows_out.at[half, part, 0, :, 1],
            rows_in.at[half, pair_of(half, part, 0), 1],
            side_out_sem.at[half, part], side_in_sem.at[half, part],
            along(half, 0, 1),
        )

    def relay(half, part, way, rows_out):
        return remote(
            rows_out.at[half, part, 2, way],
            relayed.at[half, way, part],
            relay_out_sem.at[half, part, way], relay_in_sem.at[half, part, way],
            along(half, STEPS[way], 0),
        )

    def last(half, part, way, core):
        return remote(
            relayed.at[half, way, part, core],
            rows_in.at[half, pair_of(half, part, 2), core, way],
            last_out_sem.at[half, part, way, core], last_in_sem.at[half, part, way, core],
            along(half, STEPS[way], core),
        )

    def relays_of(part, rows_out):
        return [relay(half, part, way, rows_out) for way in range(2) for half in range(2)]

    def direct_of(part, rows_out):
        return [beside(half, part, rows_out) for half in range(2)] + [
            near(half, part, way, core, rows_out)
            for core in range(CORES) for way in range(2) for half in range(2)
        ]

    def lasts_of(part):
        return [
            last(half, part, way, core)
            for core in range(CORES) for way in range(2) for half in range(2)
        ]

    below = jnp.where(
        lax.broadcasted_iota(jnp.int32, (token_count, token_count), 0)
        > lax.broadcasted_iota(jnp.int32, (token_count, token_count), 1),
        1.0,
        0.0,
    ).astype(BF16)
    shift = slots.bit_length() - 1

    def tables(facts, experts):
        lanes = len(experts) * slots
        lane = lax.broadcasted_iota(jnp.int32, (1, lanes), 1)
        block = lax.shift_right_logical(lane, shift)
        slot = lax.bitwise_and(lane, slots - 1).astype(F32)
        named = jnp.zeros((1, lanes), jnp.int32)
        for number, expert in enumerate(experts):
            named = jnp.where(block == number, expert, named)
        named = named.astype(F32)
        facts = facts.astype(F32).T
        limit = jnp.zeros((token_count, lanes), F32)
        weight = jnp.zeros((token_count, lanes), F32)
        for pick in range(pick_count):
            hit = facts[:, pick : pick + 1] == named
            weight = jnp.where(hit, facts[:, pick_count + pick : pick_count + pick + 1], weight)
            first = 2 * pick_count + pick
            limit = jnp.where(hit, facts[:, first : first + 1], limit)
        order = dot(below, jnp.where(limit > 0.0, 1.0, 0.0).astype(BF16))
        kept = (order == slot) & (order < limit)
        return (
            jnp.where(kept, 1.0, 0.0).astype(BF16),
            jnp.where(kept, weight, 0.0).astype(BF16),
        )

    def chunk_of(part, kind):
        blocks = pl.ds(part * chunk_pairs, chunk_pairs)
        halves = [rows_in[half, blocks, :, kind].reshape(chunk_rows, wide) for half in range(2)]
        return jnp.concatenate(halves, axis=1)

    def first_half(part):
        rows = pl.ds(pl.multiple_of(part * chunk_rows, chunk_rows), chunk_rows)
        x = chunk_of(part, 0)
        gate_pre = dot(x, gate[...])
        lift_pre = dot(x, lift[...])
        sigmoid = jax.nn.sigmoid(gate_pre)
        activated = gate_pre * sigmoid
        hidden_rows[rows, :] = (activated * lift_pre).astype(BF16)
        hidden_delta = dot(chunk_of(part, 1), down_kernel[...], LAST)
        deltas[rows, :inner] = (
            hidden_delta * lift_pre * sigmoid * (1.0 + gate_pre * (1.0 - sigmoid))
        ).astype(BF16)
        deltas[rows, inner:] = (hidden_delta * activated).astype(BF16)

    def second_half(part):
        rows = pl.ds(pl.multiple_of(part * chunk_rows, chunk_rows), chunk_rows)
        blocks = pl.ds(part * chunk_pairs * CORES, chunk_pairs * CORES)
        shape = (chunk_pairs * CORES, slots)
        expert_out = dot(hidden_rows[rows, :], down_kernel[...])
        prob = jnp.sum(chunk_of(part, 1).astype(F32) * expert_out, axis=1, keepdims=True)
        prob = jnp.broadcast_to(prob, (chunk_rows, NOTE)).astype(BF16)
        back_out[blocks, :, width:] = prob.reshape(*shape, NOTE)
        route_delta = dot(deltas[rows, :inner], gate[...], LAST)
        route_delta = route_delta + dot(deltas[rows, inner:], lift[...], LAST)
        back_out[blocks, :, :width] = route_delta.astype(BF16).reshape(*shape, width)

    def first_part(rows_out):
        loads = [
            pltpu.make_async_copy(source, target, kernel_sem.at[i])
            for i, (source, target) in enumerate(
                ((gate_hbm, gate), (lift_hbm, lift), (down_hbm, down_kernel))
            )
        ]
        for load in loads:
            load.start()
        pl.semaphore_wait(barrier, len(neighbours))
        for kind in (2, 0, 1):
            for way in range(2):
                for half in range(2):
                    line_own(half, way, kind).start()

        line_experts = [
            [along(half, offset, core) for offset in range(SIDE) for core in range(CORES)]
            for half in range(2)
        ]

        def choose(part):
            for half in range(2):
                if part == 0:
                    columns = slice(half * wide, (half + 1) * wide)
                    sources = (tokens[:, columns], cotangent[:, columns])
                    known = meta[...]
                else:
                    sources = (line_rows[half, part - 1, 0], line_rows[half, part - 1, 1])
                    known = line_meta[half, part - 1]
                for kind, table in enumerate(tables(known, line_experts[half])):
                    chosen = dot(table, sources[kind], FIRST).astype(BF16)
                    chosen = chosen.reshape(SIDE, CORES, slots, wide)
                    rows_out[half, part, :, kind] = chosen
                    rows_in[half, pair_of(half, part, 0), 0, kind] = chosen[0, 0]

        def send(part, copies_of):
            for copy in copies_of(part, rows_out):
                copy.start()

        def pass_last(part):
            for copy in relays_of(part, rows_out):
                copy.wait_recv()
            for copy in lasts_of(part):
                copy.start()

        choose(0)
        for half in range(2):
            for kind in (2, 0, 1):
                line_own(half, 0, kind).wait_recv()
                line_own(half, 1, kind).wait_recv()
                line_on(half, kind).start()
        send(0, relays_of)
        send(0, direct_of)
        choose(1)
        send(1, relays_of)
        send(1, direct_of)
        choose(3)
        send(3, relays_of)
        pass_last(0)
        for half in range(2):
            for kind in range(3):
                line_on(half, kind).wait_recv()
        choose(2)
        send(2, relays_of)
        send(3, direct_of)
        send(2, direct_of)
        place[...] = tables(
            meta[...], [device(-dz, -dy, core) for dz, dy in PAIRS for core in range(CORES)]
        )[0]
        pass_last(1)
        for load in loads:
            load.wait()

        def await_rows(half, part, offset):
            if offset == 0:
                beside(half, part, rows_out).wait_recv()
            for core in range(CORES):
                if offset == 2:
                    for way in range(2):
                        last(half, part, way, core).wait_recv()
                elif offset:
                    near(half, part, 1 - STEPS.index(offset), core, rows_out).wait_recv()

        @pl.loop(0, chunks)
        def _(part):
            for number in range(chunks):

                @pl.when(part == number)
                def _():
                    if number == 1:
                        pass_last(3)
                        pass_last(2)
                    for dz, dy in PAIRS[number * chunk_pairs : (number + 1) * chunk_pairs]:
                        await_rows(0, dz, dy)
                        await_rows(1, dy, dz)

            first_half(part)

            @pl.when(part < chunks // 2)
            def _():
                second_half(part)

        for half in range(2):
            for kind in range(3):
                for way in range(2):
                    line_own(half, way, kind).wait_send()
                line_on(half, kind).wait_send()
        for part in ORDER:
            for copy in relays_of(part, rows_out) + direct_of(part, rows_out) + lasts_of(part):
                copy.wait_send()

    pl.run_scoped(first_part, pltpu.VMEM((2, SIDE, SIDE, 2, CORES, slots, wide), BF16))

    def give_back(step):
        dz, dy = PAIRS[step // CORES]
        return remote(
            back_out.at[step], back_in.at[step], back_out_sem.at[step], back_in_sem.at[step],
            device(dz, dy, step % CORES),
        )

    fraction = wide // quarter

    def term(part, half, piece):
        first = (part % fraction) * quarter
        if piece == 2:
            columns = pl.ds(pl.multiple_of(first, quarter), quarter)
            scaled = rows_in[part // fraction, :, :, 1, :, columns].reshape(row_count, quarter)
            return dot(hidden_rows[:, half * half_down : (half + 1) * half_down], scaled, FIRST)
        first += half * half_gl + piece * piece_gl
        columns = pl.ds(pl.multiple_of(first, piece_gl), piece_gl)
        x = rows_in[part // fraction, :, :, 0, :, columns].reshape(row_count, piece_gl)
        return dot(x, deltas[...], FIRST)

    def second_part(partial_gl, partial_down):
        plan = (
            (across, 0, down, None),
            (across, 1, up, None),
            (up, 0, up, None),
            (down, 1, down, None),
            (down, 0, down, 0),
            (up, 1, up, 1),
        )

        def view(gl, in_down, number, piece):
            if piece == 2:
                return in_down.at[number]
            return gl.at[number, piece * piece_gl : (piece + 1) * piece_gl]

        def pass_on(number, piece):
            return pltpu.make_async_remote_copy(
                src_ref=view(partial_gl, partial_down, number, piece),
                dst_ref=view(sums_gl, sums_down, number, piece),
                send_sem=sums_out_sem.at[number, piece],
                recv_sem=sums_in_sem.at[number, piece],
                device_id=(me, plan[number][2]),
                device_id_type=MESH,
            )

        def send_sums(numbers, before=(None, None)):
            for piece in range(3):
                for number, earlier in zip(numbers, before):
                    part, half, _, taken = plan[number]
                    value = term(part, half, piece)
                    if taken is not None:
                        pass_on(taken, piece).wait_recv()
                        value = value + view(sums_gl, sums_down, taken, piece)[...].astype(F32)
                    view(partial_gl, partial_down, number, piece)[...] = value.astype(BF16)
                    if earlier is not None:
                        pass_on(earlier, piece).wait_send()
                    pass_on(number, piece).start()

        def keep(half, piece, value, more):
            if piece == 2:
                rows = slice(half * half_down, (half + 1) * half_down)
                targets = ((down_change, value),)
            else:
                rows = slice(half * half_gl + piece * piece_gl, half * half_gl + (piece + 1) * piece_gl)
                targets = ((gate_change, value[:, :inner]), (lift_change, value[:, inner:]))
            for target, values in targets:
                target[0, rows, :] = target[0, rows, :] + values if more else values

        def take(number, half, piece):
            pass_on(number, piece).wait_recv()
            value = view(sums_gl, sums_down, number, piece)[...].astype(F32)
            keep(half, piece, value, True)

        split = CORES * len(PAIRS) // 2 - 1
        send_sums((0, 1))
        for step in BACK[:split]:
            give_back(step).start()
        pl.loop(chunks // 2, chunks)(second_half)
        for step in BACK[split:]:
            give_back(step).start()
        send_sums((3, 2), (0, 1))
        for piece in range(3):
            for half in range(2):
                keep(half, piece, term(group, half, piece), False)
        send_sums((4, 5), (3, 2))

        back_in[0] = back_out[0]

        for step in range(1, expert_count):
            give_back(step).wait_recv()

        returned = back_in[:, :, :width].reshape(row_count, width)
        tokens_grad[...] = dot(place[...], returned).astype(BF16)
        notes = back_in[:, :, width:].reshape(row_count, NOTE)
        note_row = lax.broadcasted_iota(jnp.int32, (row_count, NOTE), 0)
        note_lane = lax.broadcasted_iota(jnp.int32, (row_count, NOTE), 1)
        note_step = lax.shift_right_logical(note_row, slots.bit_length() - 1)
        notes = jnp.where(note_step == note_lane, notes.astype(F32), 0.0).astype(BF16)
        by_step = dot(place[...], notes)
        note_lane = lax.broadcasted_iota(jnp.int32, (1, NOTE), 1)
        sender = jnp.full((1, NOTE), -1, jnp.int32)
        for number in range(expert_count):
            dz, dy = PAIRS[number // CORES]
            sender = jnp.where(note_lane == number, device(-dz, -dy, number % CORES), sender)
        sender = sender.astype(F32)
        facts = meta[...].astype(F32).T
        pick_lane = lax.broadcasted_iota(jnp.int32, (token_count, pick_count), 1)
        total = jnp.zeros((token_count, pick_count), F32)
        for pick in range(pick_count):
            value = jnp.where(facts[:, pick : pick + 1] == sender, by_step, 0.0)
            value = jnp.sum(value, axis=1, keepdims=True)
            total = jnp.where(pick_lane == pick, value, total)
        total = jnp.concatenate([total, jnp.zeros((token_count, NOTE - pick_count), F32)], axis=1)
        probs_grad[...] = (total.T[:pick_count] / probs[...].astype(F32)).astype(BF16)

        for numbers in ((2, 3), (4, 5)):
            for piece in range(3):
                for half, number in enumerate(numbers):
                    take(number, half, piece)
        for number in (4, 5):
            for piece in range(3):
                pass_on(number, piece).wait_send()

        for step in range(1, expert_count):
            give_back(step).wait_send()

    pl.run_scoped(
        second_part,
        pltpu.VMEM((6, half_gl, 2 * inner), BF16),
        pltpu.VMEM((6, half_down, quarter), BF16),
    )


def shards(
    tokens, cotangent, route_ids, gate_probs, expert_rank, gate_kernel, lift_kernel, down_kernel
):
    expert_count = lax.axis_size("expert")
    group_count = lax.axis_size("dp")
    token_count, pick_count = route_ids.shape
    width = tokens.shape[1]
    inner = gate_kernel.shape[2]
    slots = token_count * pick_count // expert_count
    row_count = expert_count * slots
    quarter = width // group_count
    vmem, anywhere = pl.BlockSpec(memory_space=pltpu.VMEM), pl.BlockSpec(memory_space=pl.ANY)
    dma = pltpu.SemaphoreType.DMA
    outputs = pl.pallas_call(
        functools.partial(layer_kernel, expert_count, group_count, slots, pick_count),
        out_shape=(
            pltpu.VMEM(tokens.shape, BF16),
            pltpu.VMEM((pick_count, token_count), BF16),
            pltpu.VMEM((1, quarter, inner), F32),
            pltpu.VMEM((1, quarter, inner), F32),
            pltpu.VMEM((1, inner, quarter), F32),
        ),
        in_specs=[vmem] * 4 + [pl.BlockSpec(memory_space=pltpu.SMEM)] + [anywhere] * 3,
        out_specs=[vmem] * 5,
        scratch_shapes=[
            pltpu.VMEM((FACTS, token_count), BF16),
            pltpu.VMEM((2, SIDE - 1, 2, token_count, width // 2), BF16),
            pltpu.VMEM((2, SIDE - 1, FACTS, token_count), BF16),
            pltpu.VMEM((2, 2, SIDE, CORES, slots, width // 2), BF16),
            pltpu.VMEM((2, len(PAIRS), CORES, 2, slots, width // 2), BF16),
            pltpu.VMEM((token_count, row_count), BF16),
            pltpu.VMEM((row_count, inner), BF16),
            pltpu.VMEM((row_count, 2 * inner), BF16),
            pltpu.VMEM((width, inner), BF16),
            pltpu.VMEM((width, inner), BF16),
            pltpu.VMEM((inner, width), BF16),
            pltpu.VMEM((expert_count, slots, width + NOTE), BF16),
            pltpu.VMEM((expert_count, slots, width + NOTE), BF16),
            pltpu.VMEM((6, quarter // 2, 2 * inner), BF16),
            pltpu.VMEM((6, inner // 2, quarter), BF16),
            dma((2, 3, 3)),
            dma((2, 3, 3)),
            dma((2, SIDE, 2, CORES)),
            dma((2, SIDE, 2, CORES)),
            dma((2, SIDE)),
            dma((2, SIDE)),
            dma((2, SIDE, 2)),
            dma((2, SIDE, 2)),
            dma((2, SIDE, 2, CORES)),
            dma((2, SIDE, 2, CORES)),
            dma((expert_count,)),
            dma((expert_count,)),
            dma((3,)),
            dma((6, 3)),
            dma((6, 3)),
        ],
        compiler_params=pltpu.CompilerParams(
            collective_id=0, has_side_effects=True, vmem_limit_bytes=58 * 1024 * 1024
        ),
        cost_estimate=pl.CostEstimate(
            flops=18 * row_count * width * inner,
            bytes_accessed=16 * 1024 * 1024,
            transcendentals=row_count * inner,
        ),
    )(
        tokens, cotangent, route_ids.T, gate_probs.T, expert_rank,
        gate_kernel[0], lift_kernel[0], down_kernel[0],
    )
    return (outputs[0], outputs[1].T, *outputs[2:])


def solution(mesh):
    return jax.shard_map(
        shards,
        mesh=mesh,
        in_specs=(
            P(("expert", "dp"), None),
            P(("expert", "dp"), None),
            P(("expert", "dp"), None),
            P(("expert", "dp"), None),
            P(),
            P("expert", None, None),
            P("expert", None, None),
            P("expert", None, None),
        ),
        out_specs=(
            P(("expert", "dp"), None),
            P(("expert", "dp"), None),
            P("expert", "dp", None),
            P("expert", "dp", None),
            P("expert", None, "dp"),
        ),
        check_vma=False,
    )
```

```python
import functools

import jax
import jax.numpy as jnp
from jax import lax
from jax.experimental import pallas as pl
from jax.experimental.pallas import tpu as pltpu
from jax.sharding import PartitionSpec as P

MESH = pl.DeviceIdType.MESH
FACTS = 32
NOTE = 128
FIRST = (((0,), (0,)), ((), ()))
LAST = (((1,), (1,)), ((), ()))
F32 = jnp.float32
BF16 = jnp.bfloat16


def dot(a, b, dims=(((1,), (0,)), ((), ()))):
    return lax.dot_general(a, b, dims, preferred_element_type=F32)


ORDER = (0, 1, 3, 2)
PAIRS = tuple(
    sorted(
        ((dz, dy) for dz in ORDER for dy in ORDER),
        key=lambda pair: sorted((ORDER.index(pair[0]), ORDER.index(pair[1])), reverse=True),
    )
)
CORES = 2
BACK = (1,) + tuple(
    PAIRS.index(pair) * CORES + core
    for pairs in (
        ((0, 1), (1, 0), (0, 3), (3, 0)),
        ((1, 1), (1, 3), (3, 1)),
        ((3, 3), (0, 2), (2, 0)),
        ((2, 1), (1, 2), (2, 3), (3, 2)),
        ((2, 2),),
    )
    for core in range(CORES)
    for pair in pairs
)
SIDE = 4
STEPS = (1, 3, 2)


def layer_kernel(
    expert_count, group_count, slots, pick_count,
    tokens_hbm, cotangent_hbm, routes, probs, rank, gate_hbm, lift_hbm, down_hbm,
    tokens_grad, probs_grad, gate_change, lift_change, down_change,
    tokens, cotangent, meta, line_rows, line_meta, rows_in, place, hidden_rows, deltas,
    gate, lift, down_kernel,
    back_out, back_in, sums_gl, sums_down,
    line_out_sem, line_in_sem, near_out_sem, near_in_sem, side_out_sem, side_in_sem,
    back_out_sem, back_in_sem, kernel_sem, first_sem,
    sums_out_sem, sums_in_sem,
):
    me, group = lax.axis_index("expert"), lax.axis_index("dp")
    token_count, width = tokens.shape
    wide = width // 2
    inner = hidden_rows.shape[1]
    row_count = expert_count * slots
    quarter = width // group_count
    half_gl, half_down = quarter // 2, inner // 2
    piece_gl = half_gl // 2
    chunk_pairs = len(PAIRS) // 4
    chunk_rows = chunk_pairs * CORES * slots
    chunks = len(PAIRS) // chunk_pairs
    up, down = (group + 1) % group_count, (group + group_count - 1) % group_count
    across = (group + 2) % group_count
    my_z, my_y, my_core = me // (SIDE * CORES), (me // CORES) % SIDE, me % CORES

    def device(dz, dy, core):
        z, y = (my_z + dz) % SIDE, (my_y + dy) % SIDE
        return (z * SIDE + y) * CORES + (my_core + core) % CORES

    def along(half, offset, core):
        return device(0, offset, core) if half == 0 else device(offset, 0, core)

    def pair_of(half, part, offset):
        offset %= SIDE
        return PAIRS.index((part, offset) if half == 0 else (offset, part))

    barrier = pltpu.get_barrier_semaphore()

    neighbours = [(along(half, offset, core), group)
                  for half in range(2) for offset in STEPS for core in range(CORES)]
    neighbours += [(device(0, 0, 1), group), (me, up), (me, down)]
    for neighbour in neighbours:
        pl.semaphore_signal(barrier, inc=1, device_id=neighbour, device_id_type=MESH)

    firsts = [
        pltpu.make_async_copy(source, target, first_sem.at[i])
        for i, (source, target) in enumerate(
            ((tokens_hbm, tokens), (cotangent_hbm, cotangent))
        )
    ]
    for load in firsts:
        load.start()

    experts = routes[...]
    hot = experts == rank[0]
    for place_number in range(1, expert_count // 2):
        hot = hot | (experts == rank[place_number])
    facts = jnp.concatenate(
        [
            experts.astype(F32),
            probs[...].astype(F32),
            jnp.where(hot, float(slots), float(slots // 2)),
            jnp.zeros((FACTS - 3 * pick_count, token_count), F32),
        ],
        axis=0,
    )
    meta[...] = facts.astype(BF16)

    def remote(source, target, send, receive, expert):
        return pltpu.make_async_remote_copy(
            src_ref=source,
            dst_ref=target,
            send_sem=send,
            recv_sem=receive,
            device_id=(expert, group),
            device_id_type=MESH,
        )

    def line_own(half, way, kind):
        columns = slice(half * wide, (half + 1) * wide)
        source = (tokens.at[:, columns], cotangent.at[:, columns], meta)[kind]
        slot = -STEPS[way] % SIDE - 1
        target = line_meta.at[half, slot] if kind == 2 else line_rows.at[half, slot, kind]
        return remote(
            source, target, line_out_sem.at[half, way, kind], line_in_sem.at[half, slot, kind],
            along(1 - half, STEPS[way], 0),
        )

    def line_on(half, kind):
        way = 1 if kind == 1 else 0
        slot = -STEPS[way] % SIDE - 1
        if kind == 2:
            source, target = line_meta.at[half, slot], line_meta.at[half, 1]
        else:
            source, target = line_rows.at[half, slot, kind], line_rows.at[half, 1, kind]
        return remote(
            source, target, line_out_sem.at[half, 2, kind], line_in_sem.at[half, 1, kind],
            along(1 - half, STEPS[way], 0),
        )

    def near(half, part, way, core, rows_out):
        offset = STEPS[way]
        return remote(
            rows_out.at[half, part, offset, :, core],
            rows_in.at[half, pair_of(half, part, -offset), core],
            near_out_sem.at[half, part, way, core], near_in_sem.at[half, part, way, core],
            along(half, offset, core),
        )

    def beside(half, part, rows_out):
        return remote(
            rows_out.at[half, part, 0, :, 1],
            rows_in.at[half, pair_of(half, part, 0), 1],
            side_out_sem.at[half, part], side_in_sem.at[half, part],
            along(half, 0, 1),
        )

    def sends_of(part, rows_out):
        return [beside(half, part, rows_out) for half in range(2)] + [
            near(half, part, way, core, rows_out)
            for way in (2, 0, 1) for core in range(CORES) for half in range(2)
        ]

    below = jnp.where(
        lax.broadcasted_iota(jnp.int32, (token_count, token_count), 0)
        > lax.broadcasted_iota(jnp.int32, (token_count, token_count), 1),
        1.0,
        0.0,
    ).astype(BF16)
    shift = slots.bit_length() - 1

    def tables(facts, experts):
        lanes = len(experts) * slots
        lane = lax.broadcasted_iota(jnp.int32, (1, lanes), 1)
        block = lax.shift_right_logical(lane, shift)
        slot = lax.bitwise_and(lane, slots - 1).astype(F32)
        named = jnp.zeros((1, lanes), jnp.int32)
        for number, expert in enumerate(experts):
            named = jnp.where(block == number, expert, named)
        named = named.astype(F32)
        facts = facts.astype(F32).T
        limit = jnp.zeros((token_count, lanes), F32)
        weight = jnp.zeros((token_count, lanes), F32)
        for pick in range(pick_count):
            hit = facts[:, pick : pick + 1] == named
            weight = jnp.where(hit, facts[:, pick_count + pick : pick_count + pick + 1], weight)
            first = 2 * pick_count + pick
            limit = jnp.where(hit, facts[:, first : first + 1], limit)
        order = dot(below, jnp.where(limit > 0.0, 1.0, 0.0).astype(BF16))
        kept = (order == slot) & (order < limit)
        return (
            jnp.where(kept, 1.0, 0.0).astype(BF16),
            jnp.where(kept, weight, 0.0).astype(BF16),
        )

    def chunk_of(part, kind):
        blocks = pl.ds(part * chunk_pairs, chunk_pairs)
        halves = [rows_in[half, blocks, :, kind].reshape(chunk_rows, wide) for half in range(2)]
        return jnp.concatenate(halves, axis=1)

    def first_half(part):
        rows = pl.ds(pl.multiple_of(part * chunk_rows, chunk_rows), chunk_rows)
        x = chunk_of(part, 0)
        gate_pre = dot(x, gate[...])
        lift_pre = dot(x, lift[...])
        sigmoid = jax.nn.sigmoid(gate_pre)
        activated = gate_pre * sigmoid
        hidden_rows[rows, :] = (activated * lift_pre).astype(BF16)
        hidden_delta = dot(chunk_of(part, 1), down_kernel[...], LAST)
        deltas[rows, :inner] = (
            hidden_delta * lift_pre * sigmoid * (1.0 + gate_pre * (1.0 - sigmoid))
        ).astype(BF16)
        deltas[rows, inner:] = (hidden_delta * activated).astype(BF16)

    def second_half(part):
        rows = pl.ds(pl.multiple_of(part * chunk_rows, chunk_rows), chunk_rows)
        blocks = pl.ds(part * chunk_pairs * CORES, chunk_pairs * CORES)
        shape = (chunk_pairs * CORES, slots)
        expert_out = dot(hidden_rows[rows, :], down_kernel[...])
        prob = jnp.sum(chunk_of(part, 1).astype(F32) * expert_out, axis=1, keepdims=True)
        prob = jnp.broadcast_to(prob, (chunk_rows, NOTE)).astype(BF16)
        back_out[blocks, :, width:] = prob.reshape(*shape, NOTE)
        route_delta = dot(deltas[rows, :inner], gate[...], LAST)
        route_delta = route_delta + dot(deltas[rows, inner:], lift[...], LAST)
        back_out[blocks, :, :width] = route_delta.astype(BF16).reshape(*shape, width)

    def first_part(rows_out):
        for load in firsts:
            load.wait()
        pl.semaphore_wait(barrier, len(neighbours))
        for kind in (2, 0, 1):
            for way in range(2):
                for half in range(2):
                    line_own(half, way, kind).start()

        loads = [
            pltpu.make_async_copy(source, target, kernel_sem.at[i])
            for i, (source, target) in enumerate(
                ((gate_hbm, gate), (lift_hbm, lift), (down_hbm, down_kernel))
            )
        ]
        for load in loads:
            load.start()
        line_experts = [
            [along(half, offset, core) for offset in range(SIDE) for core in range(CORES)]
            for half in range(2)
        ]

        def choose(part):
            for half in range(2):
                if part == 0:
                    columns = slice(half * wide, (half + 1) * wide)
                    sources = (tokens[:, columns], cotangent[:, columns])
                    known = meta[...]
                else:
                    sources = (line_rows[half, part - 1, 0], line_rows[half, part - 1, 1])
                    known = line_meta[half, part - 1]
                for kind, table in enumerate(tables(known, line_experts[half])):
                    chosen = dot(table, sources[kind], FIRST).astype(BF16)
                    chosen = chosen.reshape(SIDE, CORES, slots, wide)
                    rows_out[half, part, :, kind] = chosen
                    rows_in[half, pair_of(half, part, 0), 0, kind] = chosen[0, 0]

        def send(part):
            for copy in sends_of(part, rows_out):
                copy.start()

        choose(0)
        for half in range(2):
            for kind in (2, 0, 1):
                line_own(half, 0, kind).wait_recv()
                line_own(half, 1, kind).wait_recv()
                line_on(half, kind).start()
        send(0)
        choose(1)
        send(1)
        choose(3)
        send(3)
        for half in range(2):
            for kind in range(3):
                line_on(half, kind).wait_recv()
        choose(2)
        send(2)
        place[...] = tables(
            meta[...], [device(-dz, -dy, core) for dz, dy in PAIRS for core in range(CORES)]
        )[0]
        for load in loads:
            load.wait()

        def await_rows(half, part, offset):
            if offset == 0:
                beside(half, part, rows_out).wait_recv()
            else:
                for core in range(CORES):
                    near(half, part, STEPS.index(-offset % SIDE), core, rows_out).wait_recv()

        def finish_sends():
            for half in range(2):
                for kind in range(3):
                    for way in range(2):
                        line_own(half, way, kind).wait_send()
                    line_on(half, kind).wait_send()
            for part in ORDER:
                for copy in sends_of(part, rows_out):
                    copy.wait_send()

        @pl.loop(0, chunks)
        def _(part):
            for number in range(chunks):

                @pl.when(part == number)
                def _():
                    if number == chunks - 1:
                        finish_sends()
                    for dz, dy in PAIRS[number * chunk_pairs : (number + 1) * chunk_pairs]:
                        await_rows(0, dz, dy)
                        await_rows(1, dy, dz)

            first_half(part)

            @pl.when(part < chunks // 2)
            def _():
                second_half(part)

    pl.run_scoped(first_part, pltpu.VMEM((2, SIDE, SIDE, 2, CORES, slots, wide), BF16))

    def give_back(step):
        dz, dy = PAIRS[step // CORES]
        return remote(
            back_out.at[step], back_in.at[step], back_out_sem.at[step], back_in_sem.at[step],
            device(dz, dy, step % CORES),
        )

    fraction = wide // quarter

    def term(part, half, piece):
        first = (part % fraction) * quarter
        if piece == 2:
            columns = pl.ds(pl.multiple_of(first, quarter), quarter)
            scaled = rows_in[part // fraction, :, :, 1, :, columns].reshape(row_count, quarter)
            return dot(hidden_rows[:, half * half_down : (half + 1) * half_down], scaled, FIRST)
        first += half * half_gl + piece * piece_gl
        columns = pl.ds(pl.multiple_of(first, piece_gl), piece_gl)
        x = rows_in[part // fraction, :, :, 0, :, columns].reshape(row_count, piece_gl)
        return dot(x, deltas[...], FIRST)

    def second_part(partial_gl, partial_down):
        plan = (
            (across, 0, down, None),
            (across, 1, up, None),
            (up, 0, up, None),
            (down, 1, down, None),
            (down, 0, down, 0),
            (up, 1, up, 1),
        )

        def view(gl, in_down, number, piece):
            if piece == 2:
                return in_down.at[number]
            return gl.at[number, piece * piece_gl : (piece + 1) * piece_gl]

        def pass_on(number, piece):
            return pltpu.make_async_remote_copy(
                src_ref=view(partial_gl, partial_down, number, piece),
                dst_ref=view(sums_gl, sums_down, number, piece),
                send_sem=sums_out_sem.at[number, piece],
                recv_sem=sums_in_sem.at[number, piece],
                device_id=(me, plan[number][2]),
                device_id_type=MESH,
            )

        def send_sums(numbers, before=(None, None)):
            for piece in range(3):
                for number, earlier in zip(numbers, before):
                    part, half, _, taken = plan[number]
                    value = term(part, half, piece)
                    if taken is not None:
                        pass_on(taken, piece).wait_recv()
                        value = value + view(sums_gl, sums_down, taken, piece)[...].astype(F32)
                    view(partial_gl, partial_down, number, piece)[...] = value.astype(BF16)
                    if earlier is not None:
                        pass_on(earlier, piece).wait_send()
                    pass_on(number, piece).start()

        def keep(half, piece, value, more):
            if piece == 2:
                rows = slice(half * half_down, (half + 1) * half_down)
                targets = ((down_change, value),)
            else:
                rows = slice(half * half_gl + piece * piece_gl, half * half_gl + (piece + 1) * piece_gl)
                targets = ((gate_change, value[:, :inner]), (lift_change, value[:, inner:]))
            for target, values in targets:
                target[0, rows, :] = target[0, rows, :] + values if more else values

        def take(number, half, piece):
            pass_on(number, piece).wait_recv()
            value = view(sums_gl, sums_down, number, piece)[...].astype(F32)
            keep(half, piece, value, True)

        split = CORES * len(PAIRS) // 2 - 1
        send_sums((0, 1))
        for step in BACK[:split]:
            give_back(step).start()
        pl.loop(chunks // 2, chunks)(second_half)
        for step in BACK[split:]:
            give_back(step).start()
        send_sums((3, 2), (0, 1))
        for piece in range(3):
            for half in range(2):
                keep(half, piece, term(group, half, piece), False)
        send_sums((4, 5), (3, 2))

        back_in[0] = back_out[0]

        for step in range(1, expert_count):
            give_back(step).wait_recv()

        returned = back_in[:, :, :width].reshape(row_count, width)
        tokens_grad[...] = dot(place[...], returned).astype(BF16)
        notes = back_in[:, :, width:].reshape(row_count, NOTE)
        note_row = lax.broadcasted_iota(jnp.int32, (row_count, NOTE), 0)
        note_lane = lax.broadcasted_iota(jnp.int32, (row_count, NOTE), 1)
        note_step = lax.shift_right_logical(note_row, slots.bit_length() - 1)
        notes = jnp.where(note_step == note_lane, notes.astype(F32), 0.0).astype(BF16)
        by_step = dot(place[...], notes)
        note_lane = lax.broadcasted_iota(jnp.int32, (1, NOTE), 1)
        sender = jnp.full((1, NOTE), -1, jnp.int32)
        for number in range(expert_count):
            dz, dy = PAIRS[number // CORES]
            sender = jnp.where(note_lane == number, device(-dz, -dy, number % CORES), sender)
        sender = sender.astype(F32)
        facts = meta[...].astype(F32).T
        pick_lane = lax.broadcasted_iota(jnp.int32, (token_count, pick_count), 1)
        total = jnp.zeros((token_count, pick_count), F32)
        for pick in range(pick_count):
            value = jnp.where(facts[:, pick : pick + 1] == sender, by_step, 0.0)
            value = jnp.sum(value, axis=1, keepdims=True)
            total = jnp.where(pick_lane == pick, value, total)
        total = jnp.concatenate([total, jnp.zeros((token_count, NOTE - pick_count), F32)], axis=1)
        probs_grad[...] = (total.T[:pick_count] / probs[...].astype(F32)).astype(BF16)

        for step in range(1, expert_count):
            give_back(step).wait_send()
        for numbers in ((2, 3), (4, 5)):
            for piece in range(3):
                for half, number in enumerate(numbers):
                    take(number, half, piece)
        for number in (4, 5):
            for piece in range(3):
                pass_on(number, piece).wait_send()

    pl.run_scoped(
        second_part,
        pltpu.VMEM((6, half_gl, 2 * inner), BF16),
        pltpu.VMEM((6, half_down, quarter), BF16),
    )


def shards(
    tokens, cotangent, route_ids, gate_probs, expert_rank, gate_kernel, lift_kernel, down_kernel
):
    expert_count = lax.axis_size("expert")
    group_count = lax.axis_size("dp")
    token_count, pick_count = route_ids.shape
    width = tokens.shape[1]
    inner = gate_kernel.shape[2]
    slots = token_count * pick_count // expert_count
    row_count = expert_count * slots
    quarter = width // group_count
    vmem, anywhere = pl.BlockSpec(memory_space=pltpu.VMEM), pl.BlockSpec(memory_space=pl.ANY)
    dma = pltpu.SemaphoreType.DMA
    outputs = pl.pallas_call(
        functools.partial(layer_kernel, expert_count, group_count, slots, pick_count),
        out_shape=(
            pltpu.VMEM(tokens.shape, BF16),
            pltpu.VMEM((pick_count, token_count), BF16),
            pltpu.VMEM((1, quarter, inner), F32),
            pltpu.VMEM((1, quarter, inner), F32),
            pltpu.VMEM((1, inner, quarter), F32),
        ),
        in_specs=[anywhere] * 2 + [vmem] * 2 + [pl.BlockSpec(memory_space=pltpu.SMEM)] + [anywhere] * 3,
        out_specs=[vmem] * 5,
        scratch_shapes=[
            pltpu.VMEM(tokens.shape, BF16),
            pltpu.VMEM(tokens.shape, BF16),
            pltpu.VMEM((FACTS, token_count), BF16),
            pltpu.VMEM((2, SIDE - 1, 2, token_count, width // 2), BF16),
            pltpu.VMEM((2, SIDE - 1, FACTS, token_count), BF16),
            pltpu.VMEM((2, len(PAIRS), CORES, 2, slots, width // 2), BF16),
            pltpu.VMEM((token_count, row_count), BF16),
            pltpu.VMEM((row_count, inner), BF16),
            pltpu.VMEM((row_count, 2 * inner), BF16),
            pltpu.VMEM((width, inner), BF16),
            pltpu.VMEM((width, inner), BF16),
            pltpu.VMEM((inner, width), BF16),
            pltpu.VMEM((expert_count, slots, width + NOTE), BF16),
            pltpu.VMEM((expert_count, slots, width + NOTE), BF16),
            pltpu.VMEM((6, quarter // 2, 2 * inner), BF16),
            pltpu.VMEM((6, inner // 2, quarter), BF16),
            dma((2, 3, 3)),
            dma((2, 3, 3)),
            dma((2, SIDE, 3, CORES)),
            dma((2, SIDE, 3, CORES)),
            dma((2, SIDE)),
            dma((2, SIDE)),
            dma((expert_count,)),
            dma((expert_count,)),
            dma((3,)),
            dma((2,)),
            dma((6, 3)),
            dma((6, 3)),
        ],
        compiler_params=pltpu.CompilerParams(
            collective_id=0, has_side_effects=True, vmem_limit_bytes=58 * 1024 * 1024
        ),
        cost_estimate=pl.CostEstimate(
            flops=18 * row_count * width * inner,
            bytes_accessed=16 * 1024 * 1024,
            transcendentals=row_count * inner,
        ),
    )(
        tokens, cotangent, route_ids.T, gate_probs.T, expert_rank,
        gate_kernel[0], lift_kernel[0], down_kernel[0],
    )
    return (outputs[0], outputs[1].T, *outputs[2:])


def solution(mesh):
    return jax.shard_map(
        shards,
        mesh=mesh,
        in_specs=(
            P(("expert", "dp"), None),
            P(("expert", "dp"), None),
            P(("expert", "dp"), None),
            P(("expert", "dp"), None),
            P(),
            P("expert", None, None),
            P("expert", None, None),
            P("expert", None, None),
        ),
        out_specs=(
            P(("expert", "dp"), None),
            P(("expert", "dp"), None),
            P("expert", "dp", None),
            P("expert", "dp", None),
            P("expert", None, "dp"),
        ),
        check_vma=False,
    )
```

```python
import functools

import jax
import jax.numpy as jnp
from jax import lax
from jax.experimental import pallas as pl
from jax.experimental.pallas import tpu as pltpu
from jax.sharding import PartitionSpec as P

MESH = pl.DeviceIdType.MESH
FACTS = 32
NOTE = 128
FIRST = (((0,), (0,)), ((), ()))
LAST = (((1,), (1,)), ((), ()))
F32 = jnp.float32
BF16 = jnp.bfloat16


def dot(a, b, dims=(((1,), (0,)), ((), ()))):
    return lax.dot_general(a, b, dims, preferred_element_type=F32)


ORDER = (0, 1, 3, 2)
PAIRS = tuple(
    sorted(
        ((dz, dy) for dz in ORDER for dy in ORDER),
        key=lambda pair: sorted((ORDER.index(pair[0]), ORDER.index(pair[1])), reverse=True),
    )
)
CORES = 2
BACK = (1,) + tuple(
    PAIRS.index(pair) * CORES + core
    for pairs in (
        ((0, 1), (1, 0), (0, 3), (3, 0)),
        ((1, 1), (1, 3), (3, 1)),
        ((3, 3), (0, 2), (2, 0)),
        ((2, 1), (1, 2), (2, 3), (3, 2)),
        ((2, 2),),
    )
    for core in range(CORES)
    for pair in pairs
)
PIECES = (2, 0, 1)
SIDE = 4
STEPS = (1, 3)


def layer_kernel(
    expert_count, group_count, slots, pick_count,
    tokens_hbm, cotangent_hbm, routes, probs, rank, gate_hbm, lift_hbm, down_hbm,
    tokens_grad, probs_grad, gate_change, lift_change, down_change,
    tokens, cotangent, meta, line_rows, line_meta, relayed, rows_in, place, hidden_rows, deltas,
    gate, lift, down_kernel,
    back_out, back_in, sums_gl, sums_down, partial_down,
    line_out_sem, line_in_sem, near_out_sem, near_in_sem, side_out_sem, side_in_sem,
    relay_out_sem, relay_in_sem, last_out_sem, last_in_sem, back_out_sem, back_in_sem, kernel_sem,
    first_sem,
    sums_out_sem, sums_in_sem,
):
    me, group = lax.axis_index("expert"), lax.axis_index("dp")
    token_count, width = tokens.shape
    wide = width // 2
    inner = hidden_rows.shape[1]
    row_count = expert_count * slots
    quarter = width // group_count
    half_gl, half_down = quarter // 2, inner // 2
    piece_gl = half_gl // 2
    chunk_pairs = len(PAIRS) // 4
    chunk_rows = chunk_pairs * CORES * slots
    chunks = len(PAIRS) // chunk_pairs
    up, down = (group + 1) % group_count, (group + group_count - 1) % group_count
    across = (group + 2) % group_count
    my_z, my_y, my_core = me // (SIDE * CORES), (me // CORES) % SIDE, me % CORES

    def device(dz, dy, core):
        z, y = (my_z + dz) % SIDE, (my_y + dy) % SIDE
        return (z * SIDE + y) * CORES + (my_core + core) % CORES

    def along(half, offset, core):
        return device(0, offset, core) if half == 0 else device(offset, 0, core)

    def pair_of(half, part, offset):
        offset %= SIDE
        return PAIRS.index((part, offset) if half == 0 else (offset, part))

    barrier = pltpu.get_barrier_semaphore()

    neighbours = [(along(half, offset, core), group)
                  for half in range(2) for offset in STEPS for core in range(CORES)]
    neighbours += [(device(0, 0, 1), group), (me, up), (me, down)]
    for neighbour in neighbours:
        pl.semaphore_signal(barrier, inc=1, device_id=neighbour, device_id_type=MESH)

    firsts = [
        pltpu.make_async_copy(source, target, first_sem.at[i])
        for i, (source, target) in enumerate(
            ((tokens_hbm, tokens), (cotangent_hbm, cotangent))
        )
    ]
    for load in firsts:
        load.start()

    experts = routes[...]
    hot = experts == rank[0]
    for place_number in range(1, expert_count // 2):
        hot = hot | (experts == rank[place_number])
    facts = jnp.concatenate(
        [
            experts.astype(F32),
            probs[...].astype(F32),
            jnp.where(hot, float(slots), float(slots // 2)),
            jnp.zeros((FACTS - 3 * pick_count, token_count), F32),
        ],
        axis=0,
    )
    meta[...] = facts.astype(BF16)

    def remote(source, target, send, receive, expert):
        return pltpu.make_async_remote_copy(
            src_ref=source,
            dst_ref=target,
            send_sem=send,
            recv_sem=receive,
            device_id=(expert, group),
            device_id_type=MESH,
        )

    def line_own(half, way, kind):
        columns = slice(half * wide, (half + 1) * wide)
        source = (tokens.at[:, columns], cotangent.at[:, columns], meta)[kind]
        slot = -STEPS[way] % SIDE - 1
        target = line_meta.at[half, slot] if kind == 2 else line_rows.at[half, slot, kind]
        return remote(
            source, target, line_out_sem.at[half, way, kind], line_in_sem.at[half, slot, kind],
            along(1 - half, STEPS[way], 0),
        )

    def line_on(half, kind):
        way = 1 if kind == 1 else 0
        slot = -STEPS[way] % SIDE - 1
        if kind == 2:
            source, target = line_meta.at[half, slot], line_meta.at[half, 1]
        else:
            source, target = line_rows.at[half, slot, kind], line_rows.at[half, 1, kind]
        return remote(
            source, target, line_out_sem.at[half, 2, kind], line_in_sem.at[half, 1, kind],
            along(1 - half, STEPS[way], 0),
        )

    def near(half, part, way, core, rows_out):
        offset = STEPS[way]
        return remote(
            rows_out.at[half, part, offset, :, core],
            rows_in.at[half, pair_of(half, part, -offset), core],
            near_out_sem.at[half, part, way, core], near_in_sem.at[half, part, way, core],
            along(half, offset, core),
        )

    def beside(half, part, rows_out):
        return remote(
            rows_out.at[half, part, 0, :, 1],
            rows_in.at[half, pair_of(half, part, 0), 1],
            side_out_sem.at[half, part], side_in_sem.at[half, part],
            along(half, 0, 1),
        )

    def relay(half, part, way, rows_out):
        return remote(
            rows_out.at[half, part, 2, way],
            relayed.at[half, way, part],
            relay_out_sem.at[half, part, way], relay_in_sem.at[half, part, way],
            along(half, STEPS[way], 0),
        )

    def last(half, part, way, core):
        return remote(
            relayed.at[half, way, part, core],
            rows_in.at[half, pair_of(half, part, 2), core, way],
            last_out_sem.at[half, part, way, core], last_in_sem.at[half, part, way, core],
            along(half, STEPS[way], core),
        )

    def relays_of(part, rows_out):
        return [relay(half, part, way, rows_out) for way in range(2) for half in range(2)]

    def direct_of(part, rows_out):
        return [beside(half, part, rows_out) for half in range(2)] + [
            near(half, part, way, core, rows_out)
            for core in range(CORES) for way in range(2) for half in range(2)
        ]

    def lasts_of(part):
        return [
            last(half, part, way, core)
            for core in range(CORES) for way in range(2) for half in range(2)
        ]

    below = jnp.where(
        lax.broadcasted_iota(jnp.int32, (token_count, token_count), 0)
        > lax.broadcasted_iota(jnp.int32, (token_count, token_count), 1),
        1.0,
        0.0,
    ).astype(BF16)
    shift = slots.bit_length() - 1

    def tables(facts, experts):
        lanes = len(experts) * slots
        lane = lax.broadcasted_iota(jnp.int32, (1, lanes), 1)
        block = lax.shift_right_logical(lane, shift)
        slot = lax.bitwise_and(lane, slots - 1).astype(F32)
        named = jnp.zeros((1, lanes), jnp.int32)
        for number, expert in enumerate(experts):
            named = jnp.where(block == number, expert, named)
        named = named.astype(F32)
        facts = facts.astype(F32).T
        limit = jnp.zeros((token_count, lanes), F32)
        weight = jnp.zeros((token_count, lanes), F32)
        for pick in range(pick_count):
            hit = facts[:, pick : pick + 1] == named
            weight = jnp.where(hit, facts[:, pick_count + pick : pick_count + pick + 1], weight)
            first = 2 * pick_count + pick
            limit = jnp.where(hit, facts[:, first : first + 1], limit)
        order = dot(below, jnp.where(limit > 0.0, 1.0, 0.0).astype(BF16))
        kept = (order == slot) & (order < limit)
        return (
            jnp.where(kept, 1.0, 0.0).astype(BF16),
            jnp.where(kept, weight, 0.0).astype(BF16),
        )

    def chunk_of(part, kind):
        blocks = pl.ds(part * chunk_pairs, chunk_pairs)
        halves = [rows_in[half, blocks, :, kind].reshape(chunk_rows, wide) for half in range(2)]
        return jnp.concatenate(halves, axis=1)

    def first_half(part, between):
        rows = pl.ds(pl.multiple_of(part * chunk_rows, chunk_rows), chunk_rows)
        x = chunk_of(part, 0)
        gate_pre = dot(x, gate[...])
        lift_pre = dot(x, lift[...])
        sigmoid = jax.nn.sigmoid(gate_pre)
        activated = gate_pre * sigmoid
        hidden_rows[rows, :] = (activated * lift_pre).astype(BF16)
        between()
        hidden_delta = dot(chunk_of(part, 1), down_kernel[...], LAST)
        deltas[rows, :inner] = (
            hidden_delta * lift_pre * sigmoid * (1.0 + gate_pre * (1.0 - sigmoid))
        ).astype(BF16)
        deltas[rows, inner:] = (hidden_delta * activated).astype(BF16)

    def second_half(part):
        rows = pl.ds(pl.multiple_of(part * chunk_rows, chunk_rows), chunk_rows)
        blocks = pl.ds(part * chunk_pairs * CORES, chunk_pairs * CORES)
        shape = (chunk_pairs * CORES, slots)
        expert_out = dot(hidden_rows[rows, :], down_kernel[...])
        prob = jnp.sum(chunk_of(part, 1).astype(F32) * expert_out, axis=1, keepdims=True)
        prob = jnp.broadcast_to(prob, (chunk_rows, NOTE)).astype(BF16)
        back_out[blocks, :, width:] = prob.reshape(*shape, NOTE)
        route_delta = dot(deltas[rows, :inner], gate[...], LAST)
        route_delta = route_delta + dot(deltas[rows, inner:], lift[...], LAST)
        back_out[blocks, :, :width] = route_delta.astype(BF16).reshape(*shape, width)

    fraction = wide // quarter

    def term(part, half, piece):
        first = (part % fraction) * quarter
        if piece == 2:
            columns = pl.ds(pl.multiple_of(first, quarter), quarter)
            scaled = rows_in[part // fraction, :, :, 1, :, columns].reshape(row_count, quarter)
            return dot(hidden_rows[:, half * half_down : (half + 1) * half_down], scaled, FIRST)
        first += half * half_gl + piece * piece_gl
        columns = pl.ds(pl.multiple_of(first, piece_gl), piece_gl)
        x = rows_in[part // fraction, :, :, 0, :, columns].reshape(row_count, piece_gl)
        return dot(x, deltas[...], FIRST)

    plan = (
        (across, 0, down, None),
        (across, 1, up, None),
        (up, 0, up, None),
        (down, 1, down, None),
        (down, 0, down, 0),
        (up, 1, up, 1),
    )

    def view(gl, in_down, number, piece):
        if piece == 2:
            return in_down.at[number]
        return gl.at[number, piece * piece_gl : (piece + 1) * piece_gl]

    def pass_on(number, piece, partial_gl):
        return pltpu.make_async_remote_copy(
            src_ref=view(partial_gl, partial_down, number % 4, piece),
            dst_ref=view(sums_gl, sums_down, number, piece),
            send_sem=sums_out_sem.at[number, piece],
            recv_sem=sums_in_sem.at[number, piece],
            device_id=(me, plan[number][2]),
            device_id_type=MESH,
        )

    def send_sums(partial_gl, numbers, pieces, before=(None, None)):
        for piece in pieces:
            for number, earlier in zip(numbers, before):
                part, half, _, taken = plan[number]
                value = term(part, half, piece)
                if taken is not None:
                    pass_on(taken, piece, partial_gl).wait_recv()
                    value = value + view(sums_gl, sums_down, taken, piece)[...].astype(F32)
                view(partial_gl, partial_down, number % 4, piece)[...] = value.astype(BF16)
                if earlier is not None:
                    pass_on(earlier, piece, partial_gl).wait_send()
                pass_on(number, piece, partial_gl).start()

    def first_part(rows_out):
        for load in firsts:
            load.wait()
        pl.semaphore_wait(barrier, len(neighbours))
        for kind in (2, 0, 1):
            for way in range(2):
                for half in range(2):
                    line_own(half, way, kind).start()

        loads = [
            pltpu.make_async_copy(source, target, kernel_sem.at[i])
            for i, (source, target) in enumerate(
                ((gate_hbm, gate), (lift_hbm, lift), (down_hbm, down_kernel))
            )
        ]
        for load in loads:
            load.start()
        line_experts = [
            [along(half, offset, core) for offset in range(SIDE) for core in range(CORES)]
            for half in range(2)
        ]

        def choose(part):
            for half in range(2):
                if part == 0:
                    columns = slice(half * wide, (half + 1) * wide)
                    sources = (tokens[:, columns], cotangent[:, columns])
                    known = meta[...]
                else:
                    sources = (line_rows[half, part - 1, 0], line_rows[half, part - 1, 1])
                    known = line_meta[half, part - 1]
                for kind, table in enumerate(tables(known, line_experts[half])):
                    chosen = dot(table, sources[kind], FIRST).astype(BF16)
                    chosen = chosen.reshape(SIDE, CORES, slots, wide)
                    rows_out[half, part, :, kind] = chosen
                    rows_in[half, pair_of(half, part, 0), 0, kind] = chosen[0, 0]

        def send(part, copies_of):
            for copy in copies_of(part, rows_out):
                copy.start()

        def pass_last(part):
            for copy in relays_of(part, rows_out):
                copy.wait_recv()
            for copy in lasts_of(part):
                copy.start()

        choose(0)
        for half in range(2):
            for kind in (2, 0, 1):
                line_own(half, 0, kind).wait_recv()
                line_own(half, 1, kind).wait_recv()
                line_on(half, kind).start()
        send(0, relays_of)
        send(0, direct_of)
        choose(1)
        send(1, relays_of)
        send(1, direct_of)
        choose(3)
        send(3, relays_of)
        pass_last(0)
        for half in range(2):
            for kind in range(3):
                line_on(half, kind).wait_recv()
        choose(2)
        send(2, relays_of)
        send(3, direct_of)
        send(2, direct_of)
        place[...] = tables(
            meta[...], [device(-dz, -dy, core) for dz, dy in PAIRS for core in range(CORES)]
        )[0]
        pass_last(1)
        for load in loads:
            load.wait()

        def await_rows(half, part, offset):
            if offset == 0:
                beside(half, part, rows_out).wait_recv()
            for core in range(CORES):
                if offset == 2:
                    for way in range(2):
                        last(half, part, way, core).wait_recv()
                elif offset:
                    near(half, part, 1 - STEPS.index(offset), core, rows_out).wait_recv()

        def finish_sends():
            for half in range(2):
                for kind in range(3):
                    for way in range(2):
                        line_own(half, way, kind).wait_send()
                    line_on(half, kind).wait_send()
            for part in ORDER:
                for copy in relays_of(part, rows_out) + direct_of(part, rows_out):
                    copy.wait_send()

        @pl.loop(0, chunks)
        def _(part):
            for number in range(chunks):

                @pl.when(part == number)
                def _():
                    if number == chunks - 1:
                        finish_sends()
                    if number == 1:
                        pass_last(3)
                        pass_last(2)
                    for dz, dy in PAIRS[number * chunk_pairs : (number + 1) * chunk_pairs]:
                        await_rows(0, dz, dy)
                        await_rows(1, dy, dz)

            def between():
                @pl.when(part == chunks - 1)
                def _():
                    send_sums(None, (0, 1), (2,))

            first_half(part, between)

            @pl.when(part < chunks // 2)
            def _():
                second_half(part)

    pl.run_scoped(first_part, pltpu.VMEM((2, SIDE, SIDE, 2, CORES, slots, wide), BF16))

    def give_back(step):
        dz, dy = PAIRS[step // CORES]
        return remote(
            back_out.at[step], back_in.at[step], back_out_sem.at[step], back_in_sem.at[step],
            device(dz, dy, step % CORES),
        )

    def second_part(partial_gl):
        def keep(half, piece, value, more):
            if piece == 2:
                rows = slice(half * half_down, (half + 1) * half_down)
                targets = ((down_change, value),)
            else:
                rows = slice(half * half_gl + piece * piece_gl, half * half_gl + (piece + 1) * piece_gl)
                targets = ((gate_change, value[:, :inner]), (lift_change, value[:, inner:]))
            for target, values in targets:
                target[0, rows, :] = target[0, rows, :] + values if more else values

        def take(number, half, piece):
            pass_on(number, piece, partial_gl).wait_recv()
            value = view(sums_gl, sums_down, number, piece)[...].astype(F32)
            keep(half, piece, value, True)

        split = CORES * len(PAIRS) // 2 - 1
        send_sums(partial_gl, (0, 1), (0, 1))
        for step in BACK[:split]:
            give_back(step).start()
        pl.loop(chunks // 2, chunks)(second_half)
        for step in BACK[split:]:
            give_back(step).start()
        send_sums(partial_gl, (3, 2), PIECES, (0, 1))
        for piece in range(3):
            for half in range(2):
                keep(half, piece, term(group, half, piece), False)
        send_sums(partial_gl, (4, 5), PIECES, (3, 2))

        back_in[0] = back_out[0]

        for step in range(1, expert_count):
            give_back(step).wait_recv()

        returned = back_in[:, :, :width].reshape(row_count, width)
        tokens_grad[...] = dot(place[...], returned).astype(BF16)
        notes = back_in[:, :, width:].reshape(row_count, NOTE)
        note_row = lax.broadcasted_iota(jnp.int32, (row_count, NOTE), 0)
        note_lane = lax.broadcasted_iota(jnp.int32, (row_count, NOTE), 1)
        note_step = lax.shift_right_logical(note_row, slots.bit_length() - 1)
        notes = jnp.where(note_step == note_lane, notes.astype(F32), 0.0).astype(BF16)
        by_step = dot(place[...], notes)
        note_lane = lax.broadcasted_iota(jnp.int32, (1, NOTE), 1)
        sender = jnp.full((1, NOTE), -1, jnp.int32)
        for number in range(expert_count):
            dz, dy = PAIRS[number // CORES]
            sender = jnp.where(note_lane == number, device(-dz, -dy, number % CORES), sender)
        sender = sender.astype(F32)
        facts = meta[...].astype(F32).T
        pick_lane = lax.broadcasted_iota(jnp.int32, (token_count, pick_count), 1)
        total = jnp.zeros((token_count, pick_count), F32)
        for pick in range(pick_count):
            value = jnp.where(facts[:, pick : pick + 1] == sender, by_step, 0.0)
            value = jnp.sum(value, axis=1, keepdims=True)
            total = jnp.where(pick_lane == pick, value, total)
        total = jnp.concatenate([total, jnp.zeros((token_count, NOTE - pick_count), F32)], axis=1)
        probs_grad[...] = (total.T[:pick_count] / probs[...].astype(F32)).astype(BF16)

        for step in range(1, expert_count):
            give_back(step).wait_send()
        for numbers in ((2, 3), (4, 5)):
            for piece in PIECES:
                for half, number in enumerate(numbers):
                    take(number, half, piece)
        for number in (4, 5):
            for piece in range(3):
                pass_on(number, piece, partial_gl).wait_send()

        for part in ORDER:
            for copy in lasts_of(part):
                copy.wait_send()

    pl.run_scoped(second_part, pltpu.VMEM((4, half_gl, 2 * inner), BF16))


def shards(
    tokens, cotangent, route_ids, gate_probs, expert_rank, gate_kernel, lift_kernel, down_kernel
):
    expert_count = lax.axis_size("expert")
    group_count = lax.axis_size("dp")
    token_count, pick_count = route_ids.shape
    width = tokens.shape[1]
    inner = gate_kernel.shape[2]
    slots = token_count * pick_count // expert_count
    row_count = expert_count * slots
    quarter = width // group_count
    vmem, anywhere = pl.BlockSpec(memory_space=pltpu.VMEM), pl.BlockSpec(memory_space=pl.ANY)
    dma = pltpu.SemaphoreType.DMA
    outputs = pl.pallas_call(
        functools.partial(layer_kernel, expert_count, group_count, slots, pick_count),
        out_shape=(
            pltpu.VMEM(tokens.shape, BF16),
            pltpu.VMEM((pick_count, token_count), BF16),
            pltpu.VMEM((1, quarter, inner), F32),
            pltpu.VMEM((1, quarter, inner), F32),
            pltpu.VMEM((1, inner, quarter), F32),
        ),
        in_specs=[anywhere] * 2 + [vmem] * 2 + [pl.BlockSpec(memory_space=pltpu.SMEM)] + [anywhere] * 3,
        out_specs=[vmem] * 5,
        scratch_shapes=[
            pltpu.VMEM(tokens.shape, BF16),
            pltpu.VMEM(tokens.shape, BF16),
            pltpu.VMEM((FACTS, token_count), BF16),
            pltpu.VMEM((2, SIDE - 1, 2, token_count, width // 2), BF16),
            pltpu.VMEM((2, SIDE - 1, FACTS, token_count), BF16),
            pltpu.VMEM((2, 2, SIDE, CORES, slots, width // 2), BF16),
            pltpu.VMEM((2, len(PAIRS), CORES, 2, slots, width // 2), BF16),
            pltpu.VMEM((token_count, row_count), BF16),
            pltpu.VMEM((row_count, inner), BF16),
            pltpu.VMEM((row_count, 2 * inner), BF16),
            pltpu.VMEM((width, inner), BF16),
            pltpu.VMEM((width, inner), BF16),
            pltpu.VMEM((inner, width), BF16),
            pltpu.VMEM((expert_count, slots, width + NOTE), BF16),
            pltpu.VMEM((expert_count, slots, width + NOTE), BF16),
            pltpu.VMEM((6, quarter // 2, 2 * inner), BF16),
            pltpu.VMEM((6, inner // 2, quarter), BF16),
            pltpu.VMEM((4, inner // 2, quarter), BF16),
            dma((2, 3, 3)),
            dma((2, 3, 3)),
            dma((2, SIDE, 2, CORES)),
            dma((2, SIDE, 2, CORES)),
            dma((2, SIDE)),
            dma((2, SIDE)),
            dma((2, SIDE, 2)),
            dma((2, SIDE, 2)),
            dma((2, SIDE, 2, CORES)),
            dma((2, SIDE, 2, CORES)),
            dma((expert_count,)),
            dma((expert_count,)),
            dma((3,)),
            dma((2,)),
            dma((6, 3)),
            dma((6, 3)),
        ],
        compiler_params=pltpu.CompilerParams(
            collective_id=0, has_side_effects=True, vmem_limit_bytes=58 * 1024 * 1024
        ),
        cost_estimate=pl.CostEstimate(
            flops=18 * row_count * width * inner,
            bytes_accessed=16 * 1024 * 1024,
            transcendentals=row_count * inner,
        ),
    )(
        tokens, cotangent, route_ids.T, gate_probs.T, expert_rank,
        gate_kernel[0], lift_kernel[0], down_kernel[0],
    )
    return (outputs[0], outputs[1].T, *outputs[2:])


def solution(mesh):
    return jax.shard_map(
        shards,
        mesh=mesh,
        in_specs=(
            P(("expert", "dp"), None),
            P(("expert", "dp"), None),
            P(("expert", "dp"), None),
            P(("expert", "dp"), None),
            P(),
            P("expert", None, None),
            P("expert", None, None),
            P("expert", None, None),
        ),
        out_specs=(
            P(("expert", "dp"), None),
            P(("expert", "dp"), None),
            P("expert", "dp", None),
            P("expert", "dp", None),
            P("expert", None, "dp"),
        ),
        check_vma=False,
    )
```
